512 devices in a mesh: group: 16 (over x_lo, z), expert: 32 (over y, x_hi, core).
Axes of the slice: x: 4 (x_hi: 2, x_lo: 2; x = x_hi * 2 + x_lo), y: 8, z: 8, core: 2. Of those that a mesh axis runs over, the one named last changes fastest.
Arguments:
- tokens: bfloat16 [12288, 7168], P('expert', 'group'), may hold values from -6 to 6
- expert_ids: int32 [12288, 8], P('expert'), may hold values from 0 to 383, as said below
- combine: float32 [12288, 8], P('expert'), may hold values from 0.2 to 1
- w_in: bfloat16 [32, 2, 1024, 7168], P('expert', None, None, 'group'), may hold values from -0.0625 to 0.0625
- w_down: bfloat16 [32, 1024, 7168], P('expert', None, 'group'), may hold values from -0.1875 to 0.1875
Outputs:
- layer_out: bfloat16 [12288, 7168], P('expert', 'group')
The draws below stay inside these ranges and needn't reach their ends.
Inputs may be any that keep to these rules, and one draw needn't show every extreme that they name: `expert_ids`: each row names 8 different experts of all 384. Among the 384 rows of one index of expert no expert is named by more than 18 rows, and one expert below 32 is named by exactly 18 rows in every such block.
All inputs are finite; a program needn't handle non-finite values.
Results may differ from the reference program's by a relative error of at most 0.03.
Values may be sent and summed in bfloat16 or wider, within the bound.
No kernel may reach another device: no remote copies, remote signals or barrier semaphores. Data moves between devices by JAX's collectives and lax.ppermute only.
A program may use at most 64 MiB of HBM per device.

```python
import jax
import jax.numpy as jnp
from jax import lax

D = 7168
TOP = 8
ALL_EXPERTS = 384
H_WIN = 1024
TOK_DEV = 384
EXPERTS = 32
CAP = 18
TOKENS = 12288
N_GROUP = 16
N_EXPERT = 32


def draw_expert_ids(key, part):
    key = jax.random.fold_in(key, 11)
    block_count = TOKENS // TOK_DEV
    pick_slots = TOK_DEV * TOP
    lowest = CAP // 2
    busiest = jax.random.randint(jax.random.fold_in(key, 1), (), 0, EXPERTS, dtype=jnp.int32)
    labels = jnp.arange(ALL_EXPERTS, dtype=jnp.int32)

    def one_block(block):
        block_key = jax.random.fold_in(key, block + 7)
        key_order, key_length, key_rows = jax.random.split(block_key, 3)
        scores = jax.random.randint(key_order, (ALL_EXPERTS,), 0, 2 ** 20, dtype=jnp.int32) * 512 + labels
        leading = block == 0
        scores = jnp.where(leading & (labels == ALL_EXPERTS - 1), -2, scores)
        scores = jnp.where(leading & (labels == 0), -1, scores)
        scores = jnp.where(labels == busiest, 2 ** 30, scores)
        ranking = jnp.argsort(scores, stable=True)[:ALL_EXPERTS - 1].astype(jnp.int32)
        lengths = jax.random.randint(key_length, (ALL_EXPERTS - 1,), lowest, CAP + 1, dtype=jnp.int32)
        run_ends = CAP + jnp.cumsum(lengths).astype(jnp.int32)
        position = jnp.arange(pick_slots, dtype=jnp.int32)
        run_index = jnp.searchsorted(run_ends, position, side='right').astype(jnp.int32)
        run_index = jnp.clip(run_index, 0, ALL_EXPERTS - 2)
        expert_at = jnp.where(position < CAP, busiest, ranking[run_index])
        columns = expert_at.reshape(TOP, TOK_DEV)
        shuffle = jax.random.permutation(key_rows, TOK_DEV)
        return columns[:, shuffle].T
    drawn = jax.vmap(one_block)(jnp.arange(block_count, dtype=jnp.int32))
    return drawn.reshape(TOKENS, TOP).astype(jnp.int32)


def shard_levels(rng, shape, pieces, least, top_value):
    def one(dim, blocks):
        heights = jax.random.uniform(jax.random.fold_in(jax.random.fold_in(rng, 6), dim), (blocks,), jnp.float32, least / len(pieces), top_value / len(pieces))
        return jnp.repeat(jnp.exp(heights), shape[dim] // blocks).reshape((-1,) + (1,) * (len(shape) - dim - 1))

    factor_of = one(*pieces[0])
    for cut in pieces[1:]:
        factor_of = factor_of * one(*cut)
    return factor_of


def normal_values(key, dims, deviation, most, cuts=(), held_as=jnp.bfloat16):
    gain = shard_levels(key, dims, cuts, -0.22, 0.18) if cuts else 1.0
    result = jax.random.normal(key, dims, jnp.float32) * deviation * gain
    return jnp.minimum(jnp.maximum(result, -most), most).astype(held_as)


def setup_inputs(seed: int = 0) -> dict:
    streams_of = jax.random.split(jax.random.key(seed), 6)
    return {
        "tokens": normal_values(streams_of[0], (TOKENS, D), 1.0, 6.0, ((0, 32), (1, 16))),
        "expert_ids": draw_expert_ids(jax.random.fold_in(streams_of[5], 71), 0),
        "combine": jnp.clip(0.2 + 0.8 * jax.random.uniform(streams_of[2], (TOKENS, TOP), jnp.float32) ** shard_levels(streams_of[2], (TOKENS, TOP), ((0, 32),), -0.2, 0.2), 0.2, 1.0),
        "w_in": normal_values(streams_of[3], (EXPERTS, 2, H_WIN, D), D ** -0.5, 0.0625, ((0, 32), (3, 16))),
        "w_down": normal_values(streams_of[4], (EXPERTS, H_WIN, D), H_WIN ** -0.5, 0.1875, ((0, 32), (2, 16))),
    }


def reference(tokens, expert_ids, combine, w_in, w_down):
    count = N_EXPERT * CAP
    slice_width = D // N_GROUP
    order = jnp.arange(TOKENS, dtype=jnp.int32)

    def one_expert(total, expert):
        chosen = expert_ids == expert
        weight = jnp.sum(jnp.where(chosen, combine, jnp.zeros_like(combine)), axis=1)
        score = jnp.where(jnp.any(chosen, axis=1), TOKENS - order, -order).astype(jnp.int32)
        unused, picked = lax.top_k(score, count)
        picked = picked.astype(jnp.int32)
        rows = tokens[picked].astype(jnp.float32).reshape(count, N_GROUP, slice_width)
        weights = w_in[expert].astype(jnp.float32).reshape(2, H_WIN, N_GROUP, slice_width)
        slice_sums = jnp.einsum('rgd,jhgd->grjh', rows, weights).astype(jnp.bfloat16)
        slice_sums = lax.optimization_barrier(slice_sums)
        both = jnp.sum(slice_sums.astype(jnp.float32), axis=0)
        expert_hidden = (jax.nn.silu(both[:, 0]) * both[:, 1]).astype(jnp.bfloat16)
        expert_out = jnp.dot(expert_hidden, w_down[expert], preferred_element_type=jnp.float32)
        expert_out = lax.optimization_barrier(expert_out.astype(jnp.bfloat16)).astype(jnp.float32)
        total = total.at[picked].add(weight[picked][:, None] * expert_out)
        return total, None

    routed, unused = lax.scan(one_expert, jnp.zeros((TOKENS, D), jnp.float32), jnp.arange(EXPERTS, dtype=jnp.int32))
    return routed.astype(jnp.bfloat16)
```

```python
import jax
import jax.numpy as jnp
from jax import lax
from jax.experimental import pallas as pl
from jax.experimental.pallas import tpu as pltpu
from jax.sharding import PartitionSpec as P

CAP = 18
HALF = 9
EXPERTS = 32
DEPTH = 8
PAIR = 2
WIDTH = 448
PADDED = 512
MAIN = EXPERTS * 8
ROWS = EXPERTS * HALF
F32 = jnp.float32
BF16 = jnp.bfloat16
NT = (((1,), (1,)), ((), ()))
TN = (((0,), (0,)), ((), ()))
VMEM_BYTES = 48 * 1024 * 1024


def row_of_eight(shape):
    return lax.broadcasted_iota(jnp.int32, shape, 0) & 7


def spread(count):
    row = lax.broadcasted_iota(jnp.int32, (8 * count, count), 0)
    column = lax.broadcasted_iota(jnp.int32, (8 * count, count), 1)
    return ((row >> 3) == column).astype(BF16)


def pack(main, last):
    row = row_of_eight((MAIN, 128))
    lane = lax.broadcasted_iota(jnp.int32, (MAIN, 128), 1)
    even = jnp.zeros((MAIN, 128), F32)
    odd = jnp.zeros((MAIN, 128), F32)
    for tile in range(4):
        piece = last[:, 128 * tile : 128 * tile + 128]
        even = jnp.where(row == 2 * tile, piece, even)
        odd = jnp.where(row == 2 * tile + 1, piece, odd)
    runs = odd + pltpu.roll(even, 64, 1)
    tail = jnp.where(lane < 64, main[:, 384:512], runs)
    tiles = [main[:, 128 * tile : 128 * tile + 128] for tile in range(3)] + [tail]
    return jnp.concatenate([t.reshape(EXPERTS, 8, 128) for t in tiles], axis=1).astype(BF16)


def unpack(block):
    wide = block.astype(F32)
    tiles = [wide[:, 8 * tile : 8 * tile + 8, :].reshape(MAIN, 128) for tile in range(4)]
    row = row_of_eight((MAIN, 128))
    lane = lax.broadcasted_iota(jnp.int32, (MAIN, 128), 1)
    tail = tiles[3]
    main = jnp.concatenate(tiles[:3] + [jnp.where(lane < 64, tail, 0.0)], axis=1).astype(BF16)
    turned = pltpu.roll(tail, 64, 1)
    runs = [
        jnp.where(
            (row == 2 * tile) & (lane < 64),
            turned,
            jnp.where((row == 2 * tile + 1) & (lane >= 64), tail, 0.0),
        )
        for tile in range(4)
    ]
    runs = jnp.concatenate(runs, axis=1).astype(BF16)
    last = lax.dot_general(spread(EXPERTS), runs, TN, preferred_element_type=F32).astype(BF16)
    return jnp.concatenate([main, last], axis=0)


def eightfold(x):
    return jnp.broadcast_to(x[:, None, :], (x.shape[0], 8, x.shape[1])).reshape(8 * x.shape[0], x.shape[1])


def dispatch_kernel(ids_ref, tokens_ref, send_ref, slot_ref):
    count = ids_ref.shape[1]
    label = lax.broadcasted_iota(jnp.int32, (EXPERTS, count), 0)
    chosen = jnp.zeros((EXPERTS, count), F32)
    for pick in range(ids_ref.shape[0]):
        chosen = jnp.where(ids_ref[pick : pick + 1, :] == label, 1.0, chosen)
    before = lax.broadcasted_iota(jnp.int32, (count, count), 0) < lax.broadcasted_iota(
        jnp.int32, (count, count), 1
    )
    earlier = jnp.dot(chosen.astype(BF16), before.astype(BF16), preferred_element_type=F32)
    slot = jnp.where(chosen > 0.0, earlier, -1.0)
    slot_ref[...] = slot
    every = eightfold(slot)
    place = row_of_eight(every.shape).astype(F32)
    tokens = jnp.concatenate(
        [tokens_ref[...], jnp.zeros((PADDED - WIDTH, count), BF16)], axis=0
    )
    for half in range(PAIR):
        main = (every == place + HALF * half).astype(BF16)
        last = (every == 1.0 * HALF * half + 8.0).astype(BF16)
        main = lax.dot_general(main, tokens, NT, preferred_element_type=F32)
        last = lax.dot_general(last, tokens, NT, preferred_element_type=F32)
        send_ref[EXPERTS * half : EXPERTS * half + EXPERTS] = pack(main, last)


def weights_kernel(ids_ref, combine_ref, slot_ref, high_ref, low_ref):
    slot = slot_ref[...]
    label = lax.broadcasted_iota(jnp.int32, slot.shape, 0)
    weight = jnp.zeros(slot.shape, F32)
    for pick in range(ids_ref.shape[0]):
        weight = jnp.where(
            ids_ref[pick : pick + 1, :] == label, combine_ref[pick : pick + 1, :], weight
        )
    every, each = eightfold(slot), eightfold(weight)
    place = row_of_eight(every.shape).astype(F32)
    for half in range(PAIR):
        main = jnp.where(every == place + HALF * half, each, 0.0)
        last = jnp.where(slot == 1.0 * HALF * half + 8.0, weight, 0.0)
        both = jnp.concatenate([main, last], axis=0)
        high = both.astype(BF16)
        high_ref[ROWS * half : ROWS * half + ROWS] = high
        low_ref[ROWS * half : ROWS * half + ROWS] = (both - high.astype(F32)).astype(BF16)


def gate_up_kernel(side_ref, arrived_ref, own_ref, other_ref, terms_ref, own_rows, other_rows):
    @pl.when(pl.program_id(0) == 0)
    def _():
        side = side_ref[0]
        own_rows[...] = unpack(arrived_ref[pl.ds(side * EXPERTS, EXPERTS)])
        other_rows[...] = unpack(arrived_ref[pl.ds((1 - side) * EXPERTS, EXPERTS)])

    own = jnp.concatenate([own_ref[0], own_ref[1]], axis=1)
    other = jnp.concatenate([other_ref[0], other_ref[1]], axis=1)
    terms = jnp.dot(own_rows[:, :WIDTH], own, preferred_element_type=F32)
    terms += jnp.dot(other_rows[:, :WIDTH], other, preferred_element_type=F32)
    terms_ref[0] = terms.astype(BF16)


def hidden_kernel(terms_ref, hidden_ref):
    both = terms_ref[0].astype(F32)
    for piece in range(1, DEPTH):
        both += terms_ref[piece].astype(F32)
    width = both.shape[1] // 2
    gate, up = both[:, :width], both[:, width:]
    hidden = (gate / (1.0 + jnp.exp(-gate)) * up).astype(BF16)
    for piece in range(DEPTH):
        hidden_ref[piece] = hidden


def down_kernel(side_ref, hidden_ref, own_ref, other_ref, send_ref):
    side = side_ref[0]
    hidden = jnp.concatenate([hidden_ref[piece] for piece in range(DEPTH)], axis=1)
    for ref, where in ((own_ref, side), (other_ref, 1 - side)):
        down = jnp.concatenate(
            [ref[...], jnp.zeros((PADDED - WIDTH, ref.shape[1]), BF16)], axis=0
        )
        result = lax.dot_general(hidden, down, NT, preferred_element_type=F32).astype(BF16)
        last = jnp.dot(spread(EXPERTS), result[MAIN:], preferred_element_type=F32)
        send_ref[pl.ds(where * EXPERTS, EXPERTS)] = pack(result[:MAIN].astype(F32), last)


def combine_kernel(back_ref, high_ref, low_ref, out_ref):
    rows = jnp.concatenate([unpack(back_ref[:EXPERTS]), unpack(back_ref[EXPERTS:])], axis=0)
    routed = lax.dot_general(rows, high_ref[...], TN, preferred_element_type=F32)
    routed += lax.dot_general(rows, low_ref[...], TN, preferred_element_type=F32)
    out_ref[...] = routed[:WIDTH].astype(BF16)


def call(kernel, out, **more):
    return pl.pallas_call(
        kernel,
        out_shape=out,
        compiler_params=pltpu.CompilerParams(vmem_limit_bytes=VMEM_BYTES),
        **more,
    )


def local(tokens, expert_ids, combine, w_in, w_down):
    count = tokens.shape[0]
    hidden_units = w_down.shape[1]
    block = hidden_units // DEPTH
    group = lax.axis_index("group")
    side = (group // DEPTH).astype(jnp.int32).reshape(1)
    swap = [(g, (g + DEPTH) % (PAIR * DEPTH)) for g in range(PAIR * DEPTH)]
    along_z = [[x * DEPTH + z for z in range(DEPTH)] for x in range(PAIR)]
    along_pair = [
        [(x * DEPTH + z) * EXPERTS + e for x in range(PAIR) for e in range(EXPERTS)]
        for z in range(DEPTH)
    ]
    tokens, ids, combine = tokens.T, expert_ids.T, combine.T
    w_in = jnp.swapaxes(w_in[0], 1, 2)
    w_down = w_down[0].T
    scalar = pl.BlockSpec(memory_space=pltpu.SMEM)
    whole = pl.BlockSpec(memory_space=pltpu.VMEM)

    other_in = lax.ppermute(w_in, "group", swap)
    packed = (PAIR * EXPERTS, EXPERTS, 128)
    send, slot = call(
        dispatch_kernel,
        (jax.ShapeDtypeStruct(packed, BF16), jax.ShapeDtypeStruct((EXPERTS, count), F32)),
    )(ids, tokens)
    arrived = lax.all_to_all(
        send, ("group", "expert"), 0, 0, axis_index_groups=along_pair, tiled=True
    )
    high, low = call(
        weights_kernel, (jax.ShapeDtypeStruct((PAIR * ROWS, count), BF16),) * 2
    )(ids, combine, slot)
    w_down_sent, arrived = lax.optimization_barrier((w_down, arrived))
    other_down = lax.ppermute(w_down_sent, "group", swap)

    weight_spec = pl.BlockSpec((2, WIDTH, block), lambda z: (0, 0, z))
    terms = call(
        gate_up_kernel,
        jax.ShapeDtypeStruct((DEPTH, ROWS, 2 * block), BF16),
        grid=(DEPTH,),
        in_specs=[scalar, whole, weight_spec, weight_spec],
        out_specs=pl.BlockSpec((1, ROWS, 2 * block), lambda z: (z, 0, 0)),
        scratch_shapes=[pltpu.VMEM((ROWS, PADDED), BF16)] * 2,
    )(side, arrived, w_in, other_in)
    terms = lax.all_to_all(terms, "group", 0, 0, axis_index_groups=along_z, tiled=True)
    hidden = call(hidden_kernel, jax.ShapeDtypeStruct((DEPTH, ROWS, block), BF16))(terms)
    hidden = lax.all_to_all(hidden, "group", 0, 0, axis_index_groups=along_z, tiled=True)
    send = call(
        down_kernel,
        jax.ShapeDtypeStruct(packed, BF16),
        in_specs=[scalar, whole, whole, whole],
    )(side, hidden, w_down, other_down)
    back = lax.all_to_all(
        send, ("group", "expert"), 0, 0, axis_index_groups=along_pair, tiled=True
    )
    routed = call(combine_kernel, jax.ShapeDtypeStruct((WIDTH, count), BF16))(back, high, low)
    return routed.T


def solution(mesh):
    placed = (
        P("expert", "group"),
        P("expert", None),
        P("expert", None),
        P("expert", None, None, "group"),
        P("expert", None, "group"),
    )
    return jax.shard_map(
        local, mesh=mesh, in_specs=placed, out_specs=P("expert", "group"), check_vma=False
    )
```

```python
import jax
import jax.numpy as jnp
from jax import lax
from jax.experimental import pallas as pl
from jax.experimental.pallas import tpu as pltpu
from jax.sharding import PartitionSpec as P

CAP = 18
HALF = 9
EXPERTS = 32
DEPTH = 8
PAIR = 2
WIDTH = 448
PADDED = 512
MAIN = EXPERTS * 8
ROWS = EXPERTS * HALF
F32 = jnp.float32
BF16 = jnp.bfloat16
NT = (((1,), (1,)), ((), ()))
TN = (((0,), (0,)), ((), ()))
VMEM_BYTES = 48 * 1024 * 1024


def row_of_eight(shape):
    return lax.broadcasted_iota(jnp.int32, shape, 0) & 7


def spread(count):
    row = lax.broadcasted_iota(jnp.int32, (8 * count, count), 0)
    column = lax.broadcasted_iota(jnp.int32, (8 * count, count), 1)
    return ((row >> 3) == column).astype(BF16)


def pack(main, last):
    row = row_of_eight((MAIN, 128))
    lane = lax.broadcasted_iota(jnp.int32, (MAIN, 128), 1)
    even = jnp.zeros((MAIN, 128), F32)
    odd = jnp.zeros((MAIN, 128), F32)
    for tile in range(4):
        piece = last[:, 128 * tile : 128 * tile + 128]
        even = jnp.where(row == 2 * tile, piece, even)
        odd = jnp.where(row == 2 * tile + 1, piece, odd)
    runs = odd + pltpu.roll(even, 64, 1)
    tail = jnp.where(lane < 64, main[:, 384:512], runs)
    tiles = [main[:, 128 * tile : 128 * tile + 128] for tile in range(3)] + [tail]
    return jnp.concatenate([t.reshape(EXPERTS, 8, 128) for t in tiles], axis=1).astype(BF16)


def opened(block):
    wide = block.astype(F32)
    tiles = [wide[:, 8 * tile : 8 * tile + 8, :].reshape(MAIN, 128) for tile in range(4)]
    row = row_of_eight((MAIN, 128))
    lane = lax.broadcasted_iota(jnp.int32, (MAIN, 128), 1)
    tail = tiles[3]
    main = jnp.concatenate(tiles[:3] + [jnp.where(lane < 64, tail, 0.0)], axis=1).astype(BF16)
    turned = pltpu.roll(tail, 64, 1)
    runs = [
        jnp.where(
            (row == 2 * tile) & (lane < 64),
            turned,
            jnp.where((row == 2 * tile + 1) & (lane >= 64), tail, 0.0),
        )
        for tile in range(4)
    ]
    return main, jnp.concatenate(runs, axis=1).astype(BF16)


def unpack(block):
    main, runs = opened(block)
    last = lax.dot_general(spread(EXPERTS), runs, TN, preferred_element_type=F32).astype(BF16)
    return jnp.concatenate([main, last], axis=0)


def eightfold(x):
    return jnp.broadcast_to(x[:, None, :], (x.shape[0], 8, x.shape[1])).reshape(8 * x.shape[0], x.shape[1])


def dispatch_kernel(ids_ref, tokens_ref, send_ref, slot_ref):
    count = ids_ref.shape[1]
    label = lax.broadcasted_iota(jnp.int32, (EXPERTS, count), 0)
    chosen = jnp.zeros((EXPERTS, count), F32)
    for pick in range(ids_ref.shape[0]):
        chosen = jnp.where(ids_ref[pick : pick + 1, :] == label, 1.0, chosen)
    before = lax.broadcasted_iota(jnp.int32, (count, count), 0) < lax.broadcasted_iota(
        jnp.int32, (count, count), 1
    )
    earlier = jnp.dot(chosen.astype(BF16), before.astype(BF16), preferred_element_type=F32)
    slot = jnp.where(chosen > 0.0, earlier, -1.0)
    slot_ref[...] = slot
    every = eightfold(slot)
    place = row_of_eight(every.shape).astype(F32)
    tokens = jnp.concatenate(
        [tokens_ref[...], jnp.zeros((PADDED - WIDTH, count), BF16)], axis=0
    )
    for half in range(PAIR):
        main = (every == place + HALF * half).astype(BF16)
        last = (every == 1.0 * HALF * half + 8.0).astype(BF16)
        main = lax.dot_general(main, tokens, NT, preferred_element_type=F32)
        last = lax.dot_general(last, tokens, NT, preferred_element_type=F32)
        send_ref[:, 32 * half : 32 * half + 32, :] = pack(main, last)


def weights_kernel(ids_ref, combine_ref, slot_ref, high_ref, low_ref):
    slot = slot_ref[...]
    label = lax.broadcasted_iota(jnp.int32, slot.shape, 0)
    weight = jnp.zeros(slot.shape, F32)
    for pick in range(ids_ref.shape[0]):
        weight = jnp.where(
            ids_ref[pick : pick + 1, :] == label, combine_ref[pick : pick + 1, :], weight
        )
    every, each = eightfold(slot), eightfold(weight)
    place = row_of_eight(every.shape).astype(F32)
    for half in range(PAIR):
        main = jnp.where(every == place + HALF * half, each, 0.0)
        last = jnp.where(slot == 1.0 * HALF * half + 8.0, weight, 0.0)
        both = jnp.concatenate([main, last], axis=0)
        high = both.astype(BF16)
        high_ref[ROWS * half : ROWS * half + ROWS] = high
        low_ref[ROWS * half : ROWS * half + ROWS] = (both - high.astype(F32)).astype(BF16)


def ordered(count, blocks, column, last):
    per = count // blocks
    mains = per * 8 // 9
    row = lax.broadcasted_iota(jnp.int32, (count, MAIN), 0)
    block = lax.div(row, per)
    inside = row - block * per
    if last:
        chosen = (inside >= mains) & ((column >> 3) == block * (per - mains) + inside - mains)
    else:
        chosen = (inside < mains) & (column == block * mains + inside)
    return chosen.astype(BF16)


def gate_up_kernel(side_ref, arrived_ref, w_ref, terms_ref):
    side = side_ref[0]
    column = lax.broadcasted_iota(jnp.int32, (ROWS, MAIN), 1)
    take_main = ordered(ROWS, DEPTH, column, False)
    take_last = ordered(ROWS, DEPTH, column, True)
    rows = []
    for place in range(PAIR):
        half = side if place == 0 else 1 - side
        main, runs = opened(arrived_ref[:, pl.ds(half * 32, 32), :])
        taken = jnp.dot(take_main, main, preferred_element_type=F32)
        taken += jnp.dot(take_last, runs, preferred_element_type=F32)
        rows.append(taken.astype(BF16))
    rows = jnp.concatenate(rows, axis=0)[:, :WIDTH]
    units = w_ref.shape[2]
    for index in range(2):
        for start in range(0, units, PADDED):
            part = jnp.dot(rows, w_ref[index, :, start : start + PADDED], preferred_element_type=F32)
            part = part.astype(BF16)
            for place in range(PAIR):
                at = (2 * place + index) * units + start
                terms_ref[:, at : at + PADDED] = part[ROWS * place : ROWS * place + ROWS]


def hidden_kernel(kept_ref, came_ref, hidden_ref):
    units = came_ref.shape[1] // 2
    count = came_ref.shape[0]
    mains = count * 8 // 9
    both = kept_ref[:, : 2 * units].astype(F32) + came_ref[...].astype(F32)
    gate, up = both[:, :units], both[:, units:]
    hidden = (gate / (1.0 + jnp.exp(-gate)) * up).astype(BF16)
    lasts = count - mains
    row = lax.broadcasted_iota(jnp.int32, (mains, count), 0)
    column = lax.broadcasted_iota(jnp.int32, (mains, count), 1)
    pick = (column == mains + lax.rem(row, lasts)).astype(BF16)
    again = jnp.dot(pick, hidden, preferred_element_type=F32)
    run = lax.div(lax.broadcasted_iota(jnp.int32, (mains, 128), 0), lasts)
    extra = jnp.zeros((mains, 128), F32)
    for tile in range(units // 128):
        extra = jnp.where(run == tile, again[:, 128 * tile : 128 * tile + 128], extra)
    block = jnp.concatenate([hidden[:mains], extra.astype(BF16)], axis=1)
    for piece in range(DEPTH):
        hidden_ref[piece] = block


def gathered_hidden(hidden_ref):
    mains = hidden_ref.shape[1]
    units = hidden_ref.shape[2] - 128
    lasts = EXPERTS // DEPTH
    main = jnp.concatenate([hidden_ref[piece, :, :units] for piece in range(DEPTH)], axis=0)
    extra = jnp.concatenate([hidden_ref[piece, :, units:] for piece in range(DEPTH)], axis=0)
    row = lax.broadcasted_iota(jnp.int32, extra.shape, 0)
    run = lax.div(lax.rem(row, mains), lasts)
    wide = extra.astype(F32)
    runs = jnp.concatenate(
        [jnp.where(run == tile, wide, 0.0) for tile in range(units // 128)], axis=1
    ).astype(BF16)
    source = lax.broadcasted_iota(jnp.int32, (EXPERTS, DEPTH * mains), 0)
    column = lax.broadcasted_iota(jnp.int32, (EXPERTS, DEPTH * mains), 1)
    pick = source == lax.div(column, mains) * lasts + lax.rem(column, lasts)
    last = jnp.dot(pick.astype(BF16), runs, preferred_element_type=F32).astype(BF16)
    return jnp.concatenate([main, last], axis=0)


def down_kernel(side_ref, hidden_ref, own_ref, other_ref, send_ref):
    side = side_ref[0]
    hidden = gathered_hidden(hidden_ref)
    for ref, where in ((own_ref, side), (other_ref, 1 - side)):
        down = jnp.concatenate(
            [ref[...], jnp.zeros((PADDED - WIDTH, ref.shape[1]), BF16)], axis=0
        )
        result = lax.dot_general(hidden, down, NT, preferred_element_type=F32).astype(BF16)
        last = jnp.dot(spread(EXPERTS), result[MAIN:], preferred_element_type=F32)
        send_ref[pl.ds(where * EXPERTS, EXPERTS)] = pack(result[:MAIN].astype(F32), last)


def combine_kernel(back_ref, high_ref, low_ref, out_ref):
    rows = jnp.concatenate([unpack(back_ref[:EXPERTS]), unpack(back_ref[EXPERTS:])], axis=0)
    routed = lax.dot_general(rows, high_ref[...], TN, preferred_element_type=F32)
    routed += lax.dot_general(rows, low_ref[...], TN, preferred_element_type=F32)
    out_ref[...] = routed[:WIDTH].astype(BF16)


def call(kernel, out, **more):
    return pl.pallas_call(
        kernel,
        out_shape=out,
        compiler_params=pltpu.CompilerParams(vmem_limit_bytes=VMEM_BYTES),
        **more,
    )


def local(tokens, expert_ids, combine, w_in, w_down):
    count = tokens.shape[0]
    hidden_units = w_down.shape[1]
    group = lax.axis_index("group")
    side = (group // DEPTH).astype(jnp.int32).reshape(1)
    swap = [(g, (g + DEPTH) % (PAIR * DEPTH)) for g in range(PAIR * DEPTH)]
    along_z = [[x * DEPTH + z for z in range(DEPTH)] for x in range(PAIR)]
    along_pair = [
        [(x * DEPTH + z) * EXPERTS + e for x in range(PAIR) for e in range(EXPERTS)]
        for z in range(DEPTH)
    ]
    tokens, ids, combine = tokens.T, expert_ids.T, combine.T
    w_in = jnp.swapaxes(w_in[0], 1, 2)
    w_down = w_down[0].T
    scalar = pl.BlockSpec(memory_space=pltpu.SMEM)
    whole = pl.BlockSpec(memory_space=pltpu.VMEM)

    send, slot = call(
        dispatch_kernel,
        (
            jax.ShapeDtypeStruct((EXPERTS, 64, 128), BF16),
            jax.ShapeDtypeStruct((EXPERTS, count), F32),
        ),
    )(ids, tokens)
    arrived = lax.all_to_all(send, "expert", 0, 0, tiled=True)
    high, low = call(
        weights_kernel, (jax.ShapeDtypeStruct((PAIR * ROWS, count), BF16),) * 2
    )(ids, combine, slot)
    w_down_sent, arrived = lax.optimization_barrier((w_down, arrived))
    other_down = lax.ppermute(w_down_sent, "group", swap)
    terms = call(
        gate_up_kernel,
        jax.ShapeDtypeStruct((ROWS, PAIR * 2 * hidden_units), BF16),
        in_specs=[scalar, whole, whole],
    )(side, arrived, w_in)
    terms = lax.psum_scatter(
        terms, "group", scatter_dimension=0, axis_index_groups=along_z, tiled=True
    )
    terms, other_down = lax.optimization_barrier((terms, other_down))
    came = lax.ppermute(terms[:, 2 * hidden_units :], "group", swap)
    mains = EXPERTS // DEPTH * 8
    hidden = call(
        hidden_kernel, jax.ShapeDtypeStruct((DEPTH, mains, hidden_units + 128), BF16)
    )(terms, came)
    hidden = lax.all_to_all(hidden, "group", 0, 0, axis_index_groups=along_z, tiled=True)
    send = call(
        down_kernel,
        jax.ShapeDtypeStruct((PAIR * EXPERTS, 32, 128), BF16),
        in_specs=[scalar, whole, whole, whole],
    )(side, hidden, w_down, other_down)
    back = lax.all_to_all(
        send, ("group", "expert"), 0, 0, axis_index_groups=along_pair, tiled=True
    )
    routed = call(combine_kernel, jax.ShapeDtypeStruct((WIDTH, count), BF16))(back, high, low)
    return routed.T


def solution(mesh):
    placed = (
        P("expert", "group"),
        P("expert", None),
        P("expert", None),
        P("expert", None, None, "group"),
        P("expert", None, "group"),
    )
    return jax.shard_map(
        local, mesh=mesh, in_specs=placed, out_specs=P("expert", "group"), check_vma=False
    )
```

```python
import jax
import jax.numpy as jnp
from jax import lax
from jax.experimental import pallas as pl
from jax.experimental.pallas import tpu as pltpu
from jax.sharding import PartitionSpec as P

CAP = 18
HALF = 9
EXPERTS = 32
DEPTH = 8
PAIR = 2
WIDTH = 448
PADDED = 512
MAIN = EXPERTS * 8
ROWS = EXPERTS * HALF
F32 = jnp.float32
BF16 = jnp.bfloat16
NT = (((1,), (1,)), ((), ()))
TN = (((0,), (0,)), ((), ()))
VMEM_BYTES = 48 * 1024 * 1024


def row_of_eight(shape):
    return lax.broadcasted_iota(jnp.int32, shape, 0) & 7


def spread(count):
    row = lax.broadcasted_iota(jnp.int32, (8 * count, count), 0)
    column = lax.broadcasted_iota(jnp.int32, (8 * count, count), 1)
    return ((row >> 3) == column).astype(BF16)


def pack(main, last):
    row = row_of_eight((MAIN, 128))
    lane = lax.broadcasted_iota(jnp.int32, (MAIN, 128), 1)
    even = jnp.zeros((MAIN, 128), F32)
    odd = jnp.zeros((MAIN, 128), F32)
    for tile in range(4):
        piece = last[:, 128 * tile : 128 * tile + 128]
        even = jnp.where(row == 2 * tile, piece, even)
        odd = jnp.where(row == 2 * tile + 1, piece, odd)
    runs = odd + pltpu.roll(even, 64, 1)
    tail = jnp.where(lane < 64, main[:, 384:512], runs)
    tiles = [main[:, 128 * tile : 128 * tile + 128] for tile in range(3)] + [tail]
    return jnp.concatenate([t.reshape(EXPERTS, 8, 128) for t in tiles], axis=1).astype(BF16)


def opened(block):
    wide = block.astype(F32)
    tiles = [wide[:, 8 * tile : 8 * tile + 8, :].reshape(MAIN, 128) for tile in range(4)]
    row = row_of_eight((MAIN, 128))
    lane = lax.broadcasted_iota(jnp.int32, (MAIN, 128), 1)
    tail = tiles[3]
    main = jnp.concatenate(tiles[:3] + [jnp.where(lane < 64, tail, 0.0)], axis=1).astype(BF16)
    turned = pltpu.roll(tail, 64, 1)
    runs = [
        jnp.where(
            (row == 2 * tile) & (lane < 64),
            turned,
            jnp.where((row == 2 * tile + 1) & (lane >= 64), tail, 0.0),
        )
        for tile in range(4)
    ]
    return main, jnp.concatenate(runs, axis=1).astype(BF16)


def unpack(block):
    main, runs = opened(block)
    last = lax.dot_general(spread(EXPERTS), runs, TN, preferred_element_type=F32).astype(BF16)
    return jnp.concatenate([main, last], axis=0)


def eightfold(x):
    return jnp.broadcast_to(x[:, None, :], (x.shape[0], 8, x.shape[1])).reshape(8 * x.shape[0], x.shape[1])


def halves(rows, shift):
    index = lax.broadcasted_iota(jnp.int32, (rows, 1), 0)
    return ((index >> shift) & 1) * HALF


def labels(shape):
    index = lax.broadcasted_iota(jnp.int32, shape, 0)
    return (index & (EXPERTS - PAIR)) | (index >> 5)


def dispatch_kernel(ids_ref, tokens_ref, send_ref, slot_ref):
    count = ids_ref.shape[1]
    label = labels((PAIR * EXPERTS, count))
    chosen = jnp.zeros(label.shape, F32)
    for pick in range(ids_ref.shape[0]):
        chosen = jnp.where(ids_ref[pick : pick + 1, :] == label, 1.0, chosen)
    before = lax.broadcasted_iota(jnp.int32, (count, count), 0) < lax.broadcasted_iota(
        jnp.int32, (count, count), 1
    )
    earlier = jnp.dot(chosen.astype(BF16), before.astype(BF16), preferred_element_type=F32)
    slot = jnp.where(chosen > 0.0, earlier, -1.0)
    slot_ref[...] = slot
    every = eightfold(slot)
    first = halves(every.shape[0], 3)
    place = (row_of_eight((every.shape[0], 1)) + first).astype(F32)
    tokens = jnp.concatenate(
        [tokens_ref[...], jnp.zeros((PADDED - WIDTH, count), BF16)], axis=0
    )
    main = (every == place).astype(BF16)
    last = (every == (first + 8).astype(F32)).astype(BF16)
    main = lax.dot_general(main, tokens, NT, preferred_element_type=F32)
    last = lax.dot_general(last, tokens, NT, preferred_element_type=F32)
    for chip in range(PAIR):
        rows = slice(MAIN * chip, MAIN * chip + MAIN)
        send_ref[EXPERTS * chip : EXPERTS * chip + EXPERTS] = pack(main[rows], last[rows])


def weights_kernel(ids_ref, combine_ref, slot_ref, high_ref, low_ref):
    slot = slot_ref[...]
    label = labels(slot.shape)
    weight = jnp.zeros(slot.shape, F32)
    for pick in range(ids_ref.shape[0]):
        weight = jnp.where(
            ids_ref[pick : pick + 1, :] == label, combine_ref[pick : pick + 1, :], weight
        )
    every, each = eightfold(slot), eightfold(weight)
    place = (row_of_eight((every.shape[0], 1)) + halves(every.shape[0], 3)).astype(F32)
    main = jnp.where(every == place, each, 0.0)
    last = jnp.where(slot == (halves(slot.shape[0], 0) + 8).astype(F32), weight, 0.0)
    for chip in range(PAIR):
        both = jnp.concatenate(
            [main[MAIN * chip : MAIN * chip + MAIN], last[EXPERTS * chip : EXPERTS * chip + EXPERTS]],
            axis=0,
        )
        high = both.astype(BF16)
        high_ref[ROWS * chip : ROWS * chip + ROWS] = high
        low_ref[ROWS * chip : ROWS * chip + ROWS] = (both - high.astype(F32)).astype(BF16)


def ordered(count, blocks, column, last):
    per = count // blocks
    mains = per * 8 // 9
    row = lax.broadcasted_iota(jnp.int32, (count, MAIN), 0)
    block = lax.div(row, per)
    inside = row - block * per
    if last:
        chosen = (inside >= mains) & ((column >> 3) == block * (per - mains) + inside - mains)
    else:
        chosen = (inside < mains) & (column == block * mains + inside)
    return chosen.astype(BF16)


def own_gate_up_kernel(side_ref, arrived_ref, own_ref, partial_ref, rows_ref):
    side = side_ref[0]
    column = lax.broadcasted_iota(jnp.int32, (ROWS, MAIN), 1)
    take_main = ordered(ROWS, DEPTH, column, False)
    take_last = ordered(ROWS, DEPTH, column, True)
    rows = []
    for which in (side, 1 - side):
        main, runs = opened(arrived_ref[pl.ds(which * EXPERTS, EXPERTS)])
        taken = jnp.dot(take_main, main, preferred_element_type=F32)
        taken += jnp.dot(take_last, runs, preferred_element_type=F32)
        rows.append(taken.astype(BF16))
    rows_ref[...] = rows[1]
    units = own_ref.shape[2]
    for index in range(2):
        for start in range(0, units, PADDED):
            part = jnp.dot(
                rows[0][:, :WIDTH],
                own_ref[index, :, start : start + PADDED],
                preferred_element_type=F32,
            )
            partial_ref[:, index * units + start : index * units + start + PADDED] = part


def other_gate_up_kernel(partial_ref, rows_ref, other_ref, terms_ref):
    units = other_ref.shape[2]
    for index in range(2):
        for start in range(0, units, PADDED):
            at = slice(index * units + start, index * units + start + PADDED)
            part = jnp.dot(
                rows_ref[:, :WIDTH],
                other_ref[index, :, start : start + PADDED],
                preferred_element_type=F32,
            )
            terms_ref[:, at] = (partial_ref[:, at] + part).astype(BF16)


def hidden_kernel(sums_ref, hidden_ref):
    units = sums_ref.shape[1] // 2
    count = sums_ref.shape[0]
    mains = count * 8 // 9
    both = sums_ref[...].astype(F32)
    gate, up = both[:, :units], both[:, units:]
    hidden = (gate / (1.0 + jnp.exp(-gate)) * up).astype(BF16)
    lasts = count - mains
    row = lax.broadcasted_iota(jnp.int32, (mains, count), 0)
    column = lax.broadcasted_iota(jnp.int32, (mains, count), 1)
    pick = (column == mains + lax.rem(row, lasts)).astype(BF16)
    again = jnp.dot(pick, hidden, preferred_element_type=F32)
    run = lax.div(lax.broadcasted_iota(jnp.int32, (mains, 128), 0), lasts)
    extra = jnp.zeros((mains, 128), F32)
    for tile in range(units // 128):
        extra = jnp.where(run == tile, again[:, 128 * tile : 128 * tile + 128], extra)
    block = jnp.concatenate([hidden[:mains], extra.astype(BF16)], axis=1)
    for piece in range(DEPTH):
        hidden_ref[piece] = block


def gathered_hidden(hidden_ref):
    mains = hidden_ref.shape[1]
    units = hidden_ref.shape[2] - 128
    lasts = EXPERTS // DEPTH
    main = jnp.concatenate([hidden_ref[piece, :, :units] for piece in range(DEPTH)], axis=0)
    extra = jnp.concatenate([hidden_ref[piece, :, units:] for piece in range(DEPTH)], axis=0)
    row = lax.broadcasted_iota(jnp.int32, extra.shape, 0)
    run = lax.div(lax.rem(row, mains), lasts)
    wide = extra.astype(F32)
    runs = jnp.concatenate(
        [jnp.where(run == tile, wide, 0.0) for tile in range(units // 128)], axis=1
    ).astype(BF16)
    source = lax.broadcasted_iota(jnp.int32, (EXPERTS, DEPTH * mains), 0)
    column = lax.broadcasted_iota(jnp.int32, (EXPERTS, DEPTH * mains), 1)
    pick = source == lax.div(column, mains) * lasts + lax.rem(column, lasts)
    last = jnp.dot(pick.astype(BF16), runs, preferred_element_type=F32).astype(BF16)
    return jnp.concatenate([main, last], axis=0)


def down_kernel(side_ref, hidden_ref, own_ref, other_ref, send_ref):
    side = side_ref[0]
    hidden = gathered_hidden(hidden_ref)
    for ref, where in ((own_ref, side), (other_ref, 1 - side)):
        down = jnp.concatenate(
            [ref[...], jnp.zeros((PADDED - WIDTH, ref.shape[1]), BF16)], axis=0
        )
        result = lax.dot_general(hidden, down, NT, preferred_element_type=F32).astype(BF16)
        last = jnp.dot(spread(EXPERTS), result[MAIN:], preferred_element_type=F32)
        send_ref[pl.ds(where * EXPERTS, EXPERTS)] = pack(result[:MAIN].astype(F32), last)


def combine_kernel(back_ref, high_ref, low_ref, out_ref):
    rows = jnp.concatenate([unpack(back_ref[:EXPERTS]), unpack(back_ref[EXPERTS:])], axis=0)
    routed = lax.dot_general(rows, high_ref[...], TN, preferred_element_type=F32)
    routed += lax.dot_general(rows, low_ref[...], TN, preferred_element_type=F32)
    out_ref[...] = routed[:WIDTH].astype(BF16)


def call(kernel, out, **more):
    return pl.pallas_call(
        kernel,
        out_shape=out,
        compiler_params=pltpu.CompilerParams(vmem_limit_bytes=VMEM_BYTES),
        **more,
    )


def local(tokens, expert_ids, combine, w_in, w_down):
    count = tokens.shape[0]
    hidden_units = w_down.shape[1]
    side = (lax.axis_index("expert") & 1).astype(jnp.int32).reshape(1)
    everyone = ("group", "expert")
    along_z = [[x * DEPTH + z for z in range(DEPTH)] for x in range(PAIR)]
    along_plane = [
        [(x * DEPTH + z) * EXPERTS + e for x in range(PAIR) for e in range(EXPERTS)]
        for z in range(DEPTH)
    ]
    turn = [
        ((x * DEPTH + z) * EXPERTS + 2 * y + c, (c * DEPTH + z) * EXPERTS + 2 * y + x)
        for x in range(PAIR)
        for z in range(DEPTH)
        for y in range(EXPERTS // 2)
        for c in range(2)
    ]
    cores = [(e, e ^ 1) for e in range(EXPERTS)]
    tokens, ids, combine = tokens.T, expert_ids.T, combine.T
    w_in = jnp.swapaxes(w_in[0], 1, 2)
    w_down = w_down[0].T
    scalar = pl.BlockSpec(memory_space=pltpu.SMEM)
    whole = pl.BlockSpec(memory_space=pltpu.VMEM)
    packed = (PAIR * EXPERTS, 32, 128)

    own_in = lax.ppermute(w_in, everyone, turn)
    send, slot = call(
        dispatch_kernel,
        (
            jax.ShapeDtypeStruct(packed, BF16),
            jax.ShapeDtypeStruct((PAIR * EXPERTS, count), F32),
        ),
    )(ids, tokens)
    arrived = lax.all_to_all(
        send, everyone, 0, 0, axis_index_groups=along_plane, tiled=True
    )
    high, low = call(
        weights_kernel, (jax.ShapeDtypeStruct((PAIR * ROWS, count), BF16),) * 2
    )(ids, combine, slot)
    own_in, w_down, arrived = lax.optimization_barrier((own_in, w_down, arrived))
    other_in = lax.ppermute(own_in, "expert", cores)
    own_down = lax.ppermute(w_down, everyone, turn)
    partial, rows = call(
        own_gate_up_kernel,
        (
            jax.ShapeDtypeStruct((ROWS, 2 * hidden_units), F32),
            jax.ShapeDtypeStruct((ROWS, PADDED), BF16),
        ),
        in_specs=[scalar, whole, whole],
    )(side, arrived, own_in)
    terms = call(
        other_gate_up_kernel, jax.ShapeDtypeStruct((ROWS, 2 * hidden_units), BF16)
    )(partial, rows, other_in)
    sums = lax.psum_scatter(
        terms, "group", scatter_dimension=0, axis_index_groups=along_z, tiled=True
    )
    sums, own_down = lax.optimization_barrier((sums, own_down))
    other_down = lax.ppermute(own_down, "expert", cores)
    mains = EXPERTS // DEPTH * 8
    hidden = call(
        hidden_kernel, jax.ShapeDtypeStruct((DEPTH, mains, hidden_units + 128), BF16)
    )(sums)
    hidden = lax.all_to_all(hidden, "group", 0, 0, axis_index_groups=along_z, tiled=True)
    send = call(
        down_kernel,
        jax.ShapeDtypeStruct(packed, BF16),
        in_specs=[scalar, whole, whole, whole],
    )(side, hidden, own_down, other_down)
    back = lax.all_to_all(
        send, everyone, 0, 0, axis_index_groups=along_plane, tiled=True
    )
    routed = call(combine_kernel, jax.ShapeDtypeStruct((WIDTH, count), BF16))(back, high, low)
    return routed.T


def solution(mesh):
    placed = (
        P("expert", "group"),
        P("expert", None),
        P("expert", None),
        P("expert", None, None, "group"),
        P("expert", None, "group"),
    )
    return jax.shard_map(
        local, mesh=mesh, in_specs=placed, out_specs=P("expert", "group"), check_vma=False
    )
```

```python
import jax
import jax.numpy as jnp
from jax import lax
from jax.experimental import pallas as pl
from jax.experimental.pallas import tpu as pltpu
from jax.sharding import PartitionSpec as P

CAP = 18
HALF = 9
EXPERTS = 32
DEPTH = 8
PAIR = 2
WIDTH = 448
PADDED = 512
MAIN = EXPERTS * 8
ROWS = EXPERTS * HALF
SHARD = 39
F32 = jnp.float32
BF16 = jnp.bfloat16
NT = (((1,), (1,)), ((), ()))
TN = (((0,), (0,)), ((), ()))
VMEM_BYTES = 32 * 1024 * 1024


def row_of_eight(shape):
    return lax.broadcasted_iota(jnp.int32, shape, 0) & 7


def spread(count):
    row = lax.broadcasted_iota(jnp.int32, (8 * count, count), 0)
    column = lax.broadcasted_iota(jnp.int32, (8 * count, count), 1)
    return ((row >> 3) == column).astype(BF16)


def pack(main, last):
    row = row_of_eight((MAIN, 128))
    lane = lax.broadcasted_iota(jnp.int32, (MAIN, 128), 1)
    even = jnp.zeros((MAIN, 128), F32)
    odd = jnp.zeros((MAIN, 128), F32)
    for tile in range(4):
        piece = last[:, 128 * tile : 128 * tile + 128]
        even = jnp.where(row == 2 * tile, piece, even)
        odd = jnp.where(row == 2 * tile + 1, piece, odd)
    runs = odd + pltpu.roll(even, 64, 1)
    tail = jnp.where(lane < 64, main[:, 384:512], runs)
    tiles = [main[:, 128 * tile : 128 * tile + 128] for tile in range(3)] + [tail]
    return jnp.concatenate([t.reshape(EXPERTS, 8, 128) for t in tiles], axis=1).astype(BF16)


def opened(block):
    wide = block.astype(F32)
    tiles = [wide[:, 8 * tile : 8 * tile + 8, :].reshape(MAIN, 128) for tile in range(4)]
    row = row_of_eight((MAIN, 128))
    lane = lax.broadcasted_iota(jnp.int32, (MAIN, 128), 1)
    tail = tiles[3]
    main = jnp.concatenate(tiles[:3] + [jnp.where(lane < 64, tail, 0.0)], axis=1).astype(BF16)
    turned = pltpu.roll(tail, 64, 1)
    runs = [
        jnp.where(
            (row == 2 * tile) & (lane < 64),
            turned,
            jnp.where((row == 2 * tile + 1) & (lane >= 64), tail, 0.0),
        )
        for tile in range(4)
    ]
    return main, jnp.concatenate(runs, axis=1).astype(BF16)


def unpack(block):
    main, runs = opened(block)
    last = lax.dot_general(spread(EXPERTS), runs, TN, preferred_element_type=F32).astype(BF16)
    return jnp.concatenate([main, last], axis=0)


def eightfold(x):
    return jnp.broadcast_to(x[:, None, :], (x.shape[0], 8, x.shape[1])).reshape(8 * x.shape[0], x.shape[1])


def halves(rows, shift):
    index = lax.broadcasted_iota(jnp.int32, (rows, 1), 0)
    return ((index >> shift) & 1) * HALF


def labels(shape):
    index = lax.broadcasted_iota(jnp.int32, shape, 0)
    return (index & (EXPERTS - PAIR)) | (index >> 5)


def dispatch_kernel(ids_hbm, tokens_hbm, send_ref, slot_ref, ids_ref, tokens_ref, ids_sem, tokens_sem):
    ids_copy = pltpu.make_async_copy(ids_hbm, ids_ref, ids_sem)
    tokens_copy = pltpu.make_async_copy(tokens_hbm, tokens_ref, tokens_sem)
    ids_copy.start()
    tokens_copy.start()
    count = ids_ref.shape[1]
    ids_copy.wait()
    label = labels((PAIR * EXPERTS, count))
    chosen = jnp.zeros(label.shape, F32)
    for pick in range(ids_ref.shape[0]):
        chosen = jnp.where(ids_ref[pick : pick + 1, :] == label, 1.0, chosen)
    before = lax.broadcasted_iota(jnp.int32, (count, count), 0) < lax.broadcasted_iota(
        jnp.int32, (count, count), 1
    )
    earlier = jnp.dot(chosen.astype(BF16), before.astype(BF16), preferred_element_type=F32)
    slot = jnp.where(chosen > 0.0, earlier, -1.0)
    slot_ref[...] = slot
    every = eightfold(slot)
    first = halves(every.shape[0], 3)
    place = (row_of_eight((every.shape[0], 1)) + first).astype(F32)
    tokens_copy.wait()
    tokens = jnp.concatenate(
        [tokens_ref[...], jnp.zeros((PADDED - WIDTH, count), BF16)], axis=0
    )
    main = (every == place).astype(BF16)
    last = (every == (first + 8).astype(F32)).astype(BF16)
    main = lax.dot_general(main, tokens, NT, preferred_element_type=F32)
    last = lax.dot_general(last, tokens, NT, preferred_element_type=F32)
    for chip in range(PAIR):
        rows = slice(MAIN * chip, MAIN * chip + MAIN)
        send_ref[EXPERTS * chip : EXPERTS * chip + EXPERTS] = pack(main[rows], last[rows])


def weights_kernel(ids_ref, combine_ref, slot_ref, weights_ref):
    slot = slot_ref[...]
    label = labels(slot.shape)
    weight = jnp.zeros(slot.shape, F32)
    for pick in range(ids_ref.shape[0]):
        weight = jnp.where(
            ids_ref[pick : pick + 1, :] == label, combine_ref[pick : pick + 1, :], weight
        )
    every, each = eightfold(slot), eightfold(weight)
    place = (row_of_eight((every.shape[0], 1)) + halves(every.shape[0], 3)).astype(F32)
    main = jnp.where(every == place, each, 0.0)
    last = jnp.where(slot == (halves(slot.shape[0], 0) + 8).astype(F32), weight, 0.0)
    for chip in range(PAIR):
        both = jnp.concatenate(
            [main[MAIN * chip : MAIN * chip + MAIN], last[EXPERTS * chip : EXPERTS * chip + EXPERTS]],
            axis=0,
        )
        high = both.astype(BF16)
        low = (both - high.astype(F32)).astype(BF16)
        weights_ref[ROWS * chip : ROWS * chip + ROWS] = jnp.concatenate([high, low], axis=1)


def ordered(count, blocks, column, last):
    per = count // blocks
    lasts = EXPERTS // blocks
    mains = lasts * 8
    row = lax.broadcasted_iota(jnp.int32, (count, MAIN), 0)
    block = lax.div(row, per)
    inside = row - block * per
    if last:
        chosen = (
            (inside >= mains)
            & (inside < mains + lasts)
            & ((column >> 3) == block * lasts + inside - mains)
        )
    else:
        chosen = (inside < mains) & (column == block * mains + inside)
    return chosen.astype(BF16)


def own_gate_up_kernel(side_ref, arrived_ref, own_ref, partial_ref, rows_ref):
    side = side_ref[0]
    column = lax.broadcasted_iota(jnp.int32, (SHARD * DEPTH, MAIN), 1)
    take_main = ordered(SHARD * DEPTH, DEPTH, column, False)
    take_last = ordered(SHARD * DEPTH, DEPTH, column, True)
    rows = []
    for which in (side, 1 - side):
        main, runs = opened(arrived_ref[pl.ds(which * EXPERTS, EXPERTS)])
        taken = jnp.dot(take_main, main, preferred_element_type=F32)
        taken += jnp.dot(take_last, runs, preferred_element_type=F32)
        rows.append(taken.astype(BF16))
    rows_ref[...] = rows[1]
    units = own_ref.shape[2]
    for index in range(2):
        for start in range(0, units, PADDED):
            part = jnp.dot(
                rows[0][:, :WIDTH],
                own_ref[index, :, start : start + PADDED],
                preferred_element_type=F32,
            )
            partial_ref[:, index * units + start : index * units + start + PADDED] = part


def other_gate_up_kernel(partial_ref, rows_ref, other_ref, terms_ref):
    units = other_ref.shape[2]
    for index in range(2):
        for start in range(0, units, PADDED):
            at = slice(index * units + start, index * units + start + PADDED)
            part = jnp.dot(
                rows_ref[:, :WIDTH],
                other_ref[index, :, start : start + PADDED],
                preferred_element_type=F32,
            )
            terms_ref[:, at] = (partial_ref[:, at] + part).astype(BF16)


def hidden_kernel(sums_ref, hidden_ref):
    units = sums_ref.shape[1] // 2
    count = sums_ref.shape[0]
    lasts = EXPERTS // DEPTH
    mains = lasts * 8
    both = sums_ref[...].astype(F32)
    gate, up = both[:, :units], both[:, units:]
    hidden = (gate / (1.0 + jnp.exp(-gate)) * up).astype(BF16)
    row = lax.broadcasted_iota(jnp.int32, (mains, count), 0)
    column = lax.broadcasted_iota(jnp.int32, (mains, count), 1)
    pick = (column == mains + lax.rem(row, lasts)).astype(BF16)
    again = jnp.dot(pick, hidden, preferred_element_type=F32)
    run = lax.div(lax.broadcasted_iota(jnp.int32, (mains, 128), 0), lasts)
    extra = jnp.zeros((mains, 128), F32)
    for tile in range(units // 128):
        extra = jnp.where(run == tile, again[:, 128 * tile : 128 * tile + 128], extra)
    block = jnp.concatenate([hidden[:mains], extra.astype(BF16)], axis=1)
    for piece in range(DEPTH):
        hidden_ref[piece] = block


def gathered_hidden(hidden_ref):
    mains = hidden_ref.shape[1]
    units = hidden_ref.shape[2] - 128
    lasts = EXPERTS // DEPTH
    main = jnp.concatenate([hidden_ref[piece, :, :units] for piece in range(DEPTH)], axis=0)
    extra = jnp.concatenate([hidden_ref[piece, :, units:] for piece in range(DEPTH)], axis=0)
    row = lax.broadcasted_iota(jnp.int32, extra.shape, 0)
    run = lax.div(lax.rem(row, mains), lasts)
    wide = extra.astype(F32)
    runs = jnp.concatenate(
        [jnp.where(run == tile, wide, 0.0) for tile in range(units // 128)], axis=1
    ).astype(BF16)
    source = lax.broadcasted_iota(jnp.int32, (EXPERTS, DEPTH * mains), 0)
    column = lax.broadcasted_iota(jnp.int32, (EXPERTS, DEPTH * mains), 1)
    pick = source == lax.div(column, mains) * lasts + lax.rem(column, lasts)
    last = jnp.dot(pick.astype(BF16), runs, preferred_element_type=F32).astype(BF16)
    return jnp.concatenate([main, last], axis=0)


def down_kernel(side_ref, hidden_ref, own_ref, other_ref, send_ref):
    side = side_ref[0]
    hidden = gathered_hidden(hidden_ref)
    for ref, where in ((own_ref, side), (other_ref, 1 - side)):
        down = jnp.concatenate(
            [ref[...], jnp.zeros((PADDED - WIDTH, ref.shape[1]), BF16)], axis=0
        )
        result = lax.dot_general(hidden, down, NT, preferred_element_type=F32).astype(BF16)
        last = jnp.dot(spread(EXPERTS), result[MAIN:], preferred_element_type=F32)
        send_ref[pl.ds(where * EXPERTS, EXPERTS)] = pack(result[:MAIN].astype(F32), last)


def combine_kernel(back_ref, weights_ref, out_ref):
    rows = jnp.concatenate([unpack(back_ref[:EXPERTS]), unpack(back_ref[EXPERTS:])], axis=0)
    routed = lax.dot_general(rows, weights_ref[...], TN, preferred_element_type=F32)
    count = out_ref.shape[1]
    out_ref[...] = (routed[:WIDTH, :count] + routed[:WIDTH, count:]).astype(BF16)


def call(kernel, out, **more):
    return pl.pallas_call(
        kernel,
        out_shape=out,
        compiler_params=pltpu.CompilerParams(vmem_limit_bytes=VMEM_BYTES),
        **more,
    )


def local(tokens, expert_ids, combine, w_in, w_down):
    count = tokens.shape[0]
    hidden_units = w_down.shape[1]
    side = (lax.axis_index("expert") & 1).astype(jnp.int32).reshape(1)
    everyone = ("group", "expert")
    along_z = [[x * DEPTH + z for z in range(DEPTH)] for x in range(PAIR)]
    along_plane = [
        [(x * DEPTH + z) * EXPERTS + e for x in range(PAIR) for e in range(EXPERTS)]
        for z in range(DEPTH)
    ]
    turn = [
        ((x * DEPTH + z) * EXPERTS + 2 * y + c, (c * DEPTH + z) * EXPERTS + 2 * y + x)
        for x in range(PAIR)
        for z in range(DEPTH)
        for y in range(EXPERTS // 2)
        for c in range(2)
    ]
    cores = [(e, e ^ 1) for e in range(EXPERTS)]
    tokens, ids, combine = tokens.T, expert_ids.T, combine.T
    w_in = jnp.swapaxes(w_in[0], 1, 2)
    w_down = w_down[0].T
    scalar = pl.BlockSpec(memory_space=pltpu.SMEM)
    whole = pl.BlockSpec(memory_space=pltpu.VMEM)
    packed = (PAIR * EXPERTS, 32, 128)

    own_in = lax.ppermute(w_in, everyone, turn)
    send, slot = call(
        dispatch_kernel,
        (
            jax.ShapeDtypeStruct(packed, BF16),
            jax.ShapeDtypeStruct((PAIR * EXPERTS, count), F32),
        ),
        in_specs=[pl.BlockSpec(memory_space=pltpu.HBM)] * 2,
        scratch_shapes=[
            pltpu.VMEM(ids.shape, jnp.int32),
            pltpu.VMEM(tokens.shape, BF16),
            pltpu.SemaphoreType.DMA,
            pltpu.SemaphoreType.DMA,
        ],
    )(
        pltpu.with_memory_space_constraint(ids, pltpu.HBM),
        pltpu.with_memory_space_constraint(tokens, pltpu.HBM),
    )
    arrived = lax.all_to_all(
        send, everyone, 0, 0, axis_index_groups=along_plane, tiled=True
    )
    weights = call(weights_kernel, jax.ShapeDtypeStruct((PAIR * ROWS, 2 * count), BF16))(
        ids, combine, slot
    )
    own_in, w_down, arrived = lax.optimization_barrier((own_in, w_down, arrived))
    other_in = lax.ppermute(own_in, "expert", cores)
    own_down = lax.ppermute(w_down, everyone, turn)
    partial, rows = call(
        own_gate_up_kernel,
        (
            jax.ShapeDtypeStruct((SHARD * DEPTH, 2 * hidden_units), F32),
            jax.ShapeDtypeStruct((SHARD * DEPTH, PADDED), BF16),
        ),
        in_specs=[scalar, whole, whole],
    )(side, arrived, own_in)
    terms = call(
        other_gate_up_kernel, jax.ShapeDtypeStruct((SHARD * DEPTH, 2 * hidden_units), BF16)
    )(partial, rows, other_in)
    sums = lax.psum_scatter(
        terms, "group", scatter_dimension=0, axis_index_groups=along_z, tiled=True
    )
    sums, own_down = lax.optimization_barrier((sums, own_down))
    other_down = lax.ppermute(own_down, "expert", cores)
    mains = EXPERTS // DEPTH * 8
    hidden = call(
        hidden_kernel, jax.ShapeDtypeStruct((DEPTH, mains, hidden_units + 128), BF16)
    )(sums)
    hidden = lax.all_to_all(hidden, "group", 0, 0, axis_index_groups=along_z, tiled=True)
    send = call(
        down_kernel,
        jax.ShapeDtypeStruct(packed, BF16),
        in_specs=[scalar, whole, whole, whole],
    )(side, hidden, own_down, other_down)
    back = lax.all_to_all(
        send, everyone, 0, 0, axis_index_groups=along_plane, tiled=True
    )
    routed = call(combine_kernel, jax.ShapeDtypeStruct((WIDTH, count), BF16))(back, weights)
    return routed.T


def solution(mesh):
    placed = (
        P("expert", "group"),
        P("expert", None),
        P("expert", None),
        P("expert", None, None, "group"),
        P("expert", None, "group"),
    )
    return jax.shard_map(
        local, mesh=mesh, in_specs=placed, out_specs=P("expert", "group"), check_vma=False
    )
```

```python
import jax
import jax.numpy as jnp
from jax import lax
from jax.experimental import pallas as pl
from jax.experimental.pallas import tpu as pltpu
from jax.sharding import PartitionSpec as P

CAP = 18
HALF = 9
EXPERTS = 32
DEPTH = 8
PAIR = 2
WIDTH = 448
PADDED = 512
MAIN = EXPERTS * 8
ROWS = EXPERTS * HALF
SHARD = 39
F32 = jnp.float32
BF16 = jnp.bfloat16
NT = (((1,), (1,)), ((), ()))
TN = (((0,), (0,)), ((), ()))
VMEM_BYTES = 32 * 1024 * 1024


def row_of_eight(shape):
    return lax.broadcasted_iota(jnp.int32, shape, 0) & 7


def spread(count):
    row = lax.broadcasted_iota(jnp.int32, (8 * count, count), 0)
    column = lax.broadcasted_iota(jnp.int32, (8 * count, count), 1)
    return ((row >> 3) == column).astype(BF16)


def pack(main, last):
    row = row_of_eight((MAIN, 128))
    lane = lax.broadcasted_iota(jnp.int32, (MAIN, 128), 1)
    even = jnp.zeros((MAIN, 128), F32)
    odd = jnp.zeros((MAIN, 128), F32)
    for tile in range(4):
        piece = last[:, 128 * tile : 128 * tile + 128]
        even = jnp.where(row == 2 * tile, piece, even)
        odd = jnp.where(row == 2 * tile + 1, piece, odd)
    runs = odd + pltpu.roll(even, 64, 1)
    tail = jnp.where(lane < 64, main[:, 384:512], runs)
    tiles = [main[:, 128 * tile : 128 * tile + 128] for tile in range(3)] + [tail]
    return jnp.concatenate([t.reshape(EXPERTS, 8, 128) for t in tiles], axis=1).astype(BF16)


def opened(block):
    wide = block.astype(F32)
    tiles = [wide[:, 8 * tile : 8 * tile + 8, :].reshape(MAIN, 128) for tile in range(4)]
    row = row_of_eight((MAIN, 128))
    lane = lax.broadcasted_iota(jnp.int32, (MAIN, 128), 1)
    tail = tiles[3]
    main = jnp.concatenate(tiles[:3] + [jnp.where(lane < 64, tail, 0.0)], axis=1).astype(BF16)
    turned = pltpu.roll(tail, 64, 1)
    runs = [
        jnp.where(
            (row == 2 * tile) & (lane < 64),
            turned,
            jnp.where((row == 2 * tile + 1) & (lane >= 64), tail, 0.0),
        )
        for tile in range(4)
    ]
    return main, jnp.concatenate(runs, axis=1).astype(BF16)


def unpack(block):
    main, runs = opened(block)
    last = lax.dot_general(spread(EXPERTS), runs, TN, preferred_element_type=F32).astype(BF16)
    return jnp.concatenate([main, last], axis=0)


def eightfold(x):
    return jnp.broadcast_to(x[:, None, :], (x.shape[0], 8, x.shape[1])).reshape(8 * x.shape[0], x.shape[1])


def halves(rows, shift):
    index = lax.broadcasted_iota(jnp.int32, (rows, 1), 0)
    return ((index >> shift) & 1) * HALF


def labels(shape):
    index = lax.broadcasted_iota(jnp.int32, shape, 0)
    return (index & (EXPERTS - PAIR)) | (index >> 5)


def slots(ids_ref, label):
    count = ids_ref.shape[1]
    chosen = jnp.zeros(label.shape, F32)
    for pick in range(ids_ref.shape[0]):
        chosen = jnp.where(ids_ref[pick : pick + 1, :] == label, 1.0, chosen)
    before = lax.broadcasted_iota(jnp.int32, (count, count), 0) < lax.broadcasted_iota(
        jnp.int32, (count, count), 1
    )
    earlier = jnp.dot(chosen.astype(BF16), before.astype(BF16), preferred_element_type=F32)
    return jnp.where(chosen > 0.0, earlier, -1.0)


def dispatch_kernel(ids_hbm, tokens_hbm, send_ref, ids_ref, tokens_ref, ids_sem, tokens_sem):
    ids_copy = pltpu.make_async_copy(ids_hbm, ids_ref, ids_sem)
    tokens_copy = pltpu.make_async_copy(tokens_hbm, tokens_ref, tokens_sem)
    ids_copy.start()
    tokens_copy.start()
    count = ids_ref.shape[1]
    ids_copy.wait()
    every = eightfold(slots(ids_ref, labels((PAIR * EXPERTS, count))))
    first = halves(every.shape[0], 3)
    place = (row_of_eight((every.shape[0], 1)) + first).astype(F32)
    tokens_copy.wait()
    tokens = jnp.concatenate(
        [tokens_ref[...], jnp.zeros((PADDED - WIDTH, count), BF16)], axis=0
    )
    main = (every == place).astype(BF16)
    last = (every == (first + 8).astype(F32)).astype(BF16)
    main = lax.dot_general(main, tokens, NT, preferred_element_type=F32)
    last = lax.dot_general(last, tokens, NT, preferred_element_type=F32)
    for chip in range(PAIR):
        rows = slice(MAIN * chip, MAIN * chip + MAIN)
        send_ref[EXPERTS * chip : EXPERTS * chip + EXPERTS] = pack(main[rows], last[rows])


def weights_kernel(core_ref, ids_ref, combine_ref, weights_ref):
    core = core_ref[0]
    index = lax.broadcasted_iota(jnp.int32, (PAIR * EXPERTS, ids_ref.shape[1]), 0)
    label = 2 * (index & 15) + ((index >> 4) & 1)
    slot = slots(ids_ref, label)
    weight = jnp.zeros(slot.shape, F32)
    for pick in range(ids_ref.shape[0]):
        weight = jnp.where(
            ids_ref[pick : pick + 1, :] == label, combine_ref[pick : pick + 1, :], weight
        )
    for part in range(PAIR):
        first = (HALF * (core if part == 0 else 1 - core)).astype(F32)
        own = slice(EXPERTS * part, EXPERTS * part + EXPERTS)
        every, each = eightfold(slot[own]), eightfold(weight[own])
        place = row_of_eight((MAIN, 1)).astype(F32) + first
        main = jnp.where(every == place, each, 0.0)
        last = jnp.where(slot[own] == first + 8.0, weight[own], 0.0)
        both = jnp.concatenate([main, last], axis=0)
        high = both.astype(BF16)
        low = (both - high.astype(F32)).astype(BF16)
        weights_ref[part] = jnp.concatenate([high, low], axis=1)


def ordered(count, blocks, column, last):
    per = count // blocks
    lasts = EXPERTS // blocks
    mains = lasts * 8
    row = lax.broadcasted_iota(jnp.int32, (count, MAIN), 0)
    block = lax.div(row, per)
    inside = row - block * per
    if last:
        chosen = (
            (inside >= mains)
            & (inside < mains + lasts)
            & ((column >> 3) == block * lasts + inside - mains)
        )
    else:
        chosen = (inside < mains) & (column == block * mains + inside)
    return chosen.astype(BF16)


def own_gate_up_kernel(core_ref, arrived_ref, own_ref, partial_ref, rows_ref):
    side = 1 - core_ref[0]
    column = lax.broadcasted_iota(jnp.int32, (SHARD * DEPTH, MAIN), 1)
    take_main = ordered(SHARD * DEPTH, DEPTH, column, False)
    take_last = ordered(SHARD * DEPTH, DEPTH, column, True)
    rows = []
    for which in (side, 1 - side):
        main, runs = opened(arrived_ref[pl.ds(which * EXPERTS, EXPERTS)])
        taken = jnp.dot(take_main, main, preferred_element_type=F32)
        taken += jnp.dot(take_last, runs, preferred_element_type=F32)
        rows.append(taken.astype(BF16))
    rows_ref[...] = rows[1]
    units = own_ref.shape[2]
    for index in range(2):
        for start in range(0, units, PADDED):
            part = jnp.dot(
                rows[0][:, :WIDTH],
                own_ref[index, :, start : start + PADDED],
                preferred_element_type=F32,
            )
            partial_ref[:, index * units + start : index * units + start + PADDED] = part


def other_gate_up_kernel(partial_ref, rows_ref, other_ref, terms_ref):
    units = other_ref.shape[2]
    for index in range(2):
        for start in range(0, units, PADDED):
            at = slice(index * units + start, index * units + start + PADDED)
            part = jnp.dot(
                rows_ref[:, :WIDTH],
                other_ref[index, :, start : start + PADDED],
                preferred_element_type=F32,
            )
            terms_ref[:, at] = (partial_ref[:, at] + part).astype(BF16)


def hidden_kernel(sums_ref, hidden_ref):
    units = sums_ref.shape[1] // 2
    count = sums_ref.shape[0]
    lasts = EXPERTS // DEPTH
    mains = lasts * 8
    both = sums_ref[...].astype(F32)
    gate, up = both[:, :units], both[:, units:]
    hidden = (gate / (1.0 + jnp.exp(-gate)) * up).astype(BF16)
    row = lax.broadcasted_iota(jnp.int32, (mains, count), 0)
    column = lax.broadcasted_iota(jnp.int32, (mains, count), 1)
    pick = (column == mains + lax.rem(row, lasts)).astype(BF16)
    again = jnp.dot(pick, hidden, preferred_element_type=F32)
    run = lax.div(lax.broadcasted_iota(jnp.int32, (mains, 128), 0), lasts)
    extra = jnp.zeros((mains, 128), F32)
    for tile in range(units // 128):
        extra = jnp.where(run == tile, again[:, 128 * tile : 128 * tile + 128], extra)
    block = jnp.concatenate([hidden[:mains], extra.astype(BF16)], axis=1)
    for piece in range(DEPTH):
        hidden_ref[piece] = block


def gathered_hidden(hidden_ref):
    mains = hidden_ref.shape[1]
    units = hidden_ref.shape[2] - 128
    lasts = EXPERTS // DEPTH
    main = jnp.concatenate([hidden_ref[piece, :, :units] for piece in range(DEPTH)], axis=0)
    extra = jnp.concatenate([hidden_ref[piece, :, units:] for piece in range(DEPTH)], axis=0)
    row = lax.broadcasted_iota(jnp.int32, extra.shape, 0)
    run = lax.div(lax.rem(row, mains), lasts)
    wide = extra.astype(F32)
    runs = jnp.concatenate(
        [jnp.where(run == tile, wide, 0.0) for tile in range(units // 128)], axis=1
    ).astype(BF16)
    source = lax.broadcasted_iota(jnp.int32, (EXPERTS, DEPTH * mains), 0)
    column = lax.broadcasted_iota(jnp.int32, (EXPERTS, DEPTH * mains), 1)
    pick = source == lax.div(column, mains) * lasts + lax.rem(column, lasts)
    last = jnp.dot(pick.astype(BF16), runs, preferred_element_type=F32).astype(BF16)
    return jnp.concatenate([main, last], axis=0)


def down_kernel(core_ref, hidden_ref, own_ref, other_ref, send_ref):
    core = core_ref[0]
    hidden = gathered_hidden(hidden_ref)
    chips = EXPERTS // 2
    for ref, where in ((own_ref, 1 - core), (other_ref, core)):
        down = jnp.concatenate(
            [ref[...], jnp.zeros((PADDED - WIDTH, ref.shape[1]), BF16)], axis=0
        )
        result = lax.dot_general(hidden, down, NT, preferred_element_type=F32).astype(BF16)
        last = jnp.dot(spread(EXPERTS), result[MAIN:], preferred_element_type=F32)
        blocks = pack(result[:MAIN].astype(F32), last).reshape(chips, 2, 32, 128)
        at = pl.ds(where * chips, chips)
        send_ref[at, pl.ds(core, 1)] = blocks[:, 0:1]
        send_ref[at, pl.ds(1 - core, 1)] = blocks[:, 1:2]


def kept_kernel(back_ref, weights_ref, partial_ref):
    partial_ref[...] = lax.dot_general(
        unpack(back_ref[:, 0]), weights_ref[0], TN, preferred_element_type=F32
    )[:WIDTH]


def combine_kernel(partial_ref, came_ref, weights_ref, out_ref):
    routed = partial_ref[...]
    routed += lax.dot_general(
        unpack(came_ref[...]), weights_ref[1], TN, preferred_element_type=F32
    )[:WIDTH]
    count = out_ref.shape[1]
    out_ref[...] = (routed[:, :count] + routed[:, count:]).astype(BF16)


def call(kernel, out, **more):
    return pl.pallas_call(
        kernel,
        out_shape=out,
        compiler_params=pltpu.CompilerParams(vmem_limit_bytes=VMEM_BYTES),
        **more,
    )


def local(tokens, expert_ids, combine, w_in, w_down):
    count = tokens.shape[0]
    hidden_units = w_down.shape[1]
    core = (lax.axis_index("expert") & 1).astype(jnp.int32).reshape(1)
    everyone = ("group", "expert")
    along_z = [[x * DEPTH + z for z in range(DEPTH)] for x in range(PAIR)]
    along_plane = [
        [(x * DEPTH + z) * EXPERTS + e for x in range(PAIR) for e in range(EXPERTS)]
        for z in range(DEPTH)
    ]
    along_core = [
        [(x * DEPTH + z) * EXPERTS + 2 * y + c for x in range(PAIR) for y in range(EXPERTS // 2)]
        for z in range(DEPTH)
        for c in range(2)
    ]
    turn = [
        ((x * DEPTH + z) * EXPERTS + 2 * y + c, (c * DEPTH + z) * EXPERTS + 2 * y + 1 - x)
        for x in range(PAIR)
        for z in range(DEPTH)
        for y in range(EXPERTS // 2)
        for c in range(2)
    ]
    cores = [(e, e ^ 1) for e in range(EXPERTS)]
    tokens, ids, combine = tokens.T, expert_ids.T, combine.T
    w_in = jnp.swapaxes(w_in[0], 1, 2)
    w_down = w_down[0].T
    scalar = pl.BlockSpec(memory_space=pltpu.SMEM)
    whole = pl.BlockSpec(memory_space=pltpu.VMEM)
    packed = (PAIR * EXPERTS, 32, 128)

    own_in = lax.ppermute(w_in, everyone, turn)
    send = call(
        dispatch_kernel,
        jax.ShapeDtypeStruct(packed, BF16),
        in_specs=[pl.BlockSpec(memory_space=pltpu.HBM)] * 2,
        scratch_shapes=[
            pltpu.VMEM(ids.shape, jnp.int32),
            pltpu.VMEM(tokens.shape, BF16),
            pltpu.SemaphoreType.DMA,
            pltpu.SemaphoreType.DMA,
        ],
    )(
        pltpu.with_memory_space_constraint(ids, pltpu.HBM),
        pltpu.with_memory_space_constraint(tokens, pltpu.HBM),
    )
    arrived = lax.all_to_all(
        send, everyone, 0, 0, axis_index_groups=along_plane, tiled=True
    )
    own_in, w_down, arrived = lax.optimization_barrier((own_in, w_down, arrived))
    other_in = lax.ppermute(own_in, "expert", cores)
    own_down = lax.ppermute(w_down, everyone, turn)
    partial, rows = call(
        own_gate_up_kernel,
        (
            jax.ShapeDtypeStruct((SHARD * DEPTH, 2 * hidden_units), F32),
            jax.ShapeDtypeStruct((SHARD * DEPTH, PADDED), BF16),
        ),
        in_specs=[scalar, whole, whole],
    )(core, arrived, own_in)
    terms = call(
        other_gate_up_kernel, jax.ShapeDtypeStruct((SHARD * DEPTH, 2 * hidden_units), BF16)
    )(partial, rows, other_in)
    sums = lax.psum_scatter(
        terms, "group", scatter_dimension=0, axis_index_groups=along_z, tiled=True
    )
    sums, own_down = lax.optimization_barrier((sums, own_down))
    other_down = lax.ppermute(own_down, "expert", cores)
    mains = EXPERTS // DEPTH * 8
    hidden = call(
        hidden_kernel, jax.ShapeDtypeStruct((DEPTH, mains, hidden_units + 128), BF16)
    )(sums)
    hidden = lax.all_to_all(hidden, "group", 0, 0, axis_index_groups=along_z, tiled=True)
    send = call(
        down_kernel,
        jax.ShapeDtypeStruct((EXPERTS, 2, 32, 128), BF16),
        in_specs=[scalar, whole, whole, whole],
    )(core, hidden, own_down, other_down)
    back = lax.all_to_all(send, everyone, 0, 0, axis_index_groups=along_core, tiled=True)
    came = lax.ppermute(back[:, 1], "expert", cores)
    weights = call(
        weights_kernel,
        jax.ShapeDtypeStruct((PAIR, ROWS, 2 * count), BF16),
        in_specs=[scalar, whole, whole],
    )(core, ids, combine)
    partial = call(kept_kernel, jax.ShapeDtypeStruct((WIDTH, 2 * count), F32))(back, weights)
    routed = call(combine_kernel, jax.ShapeDtypeStruct((WIDTH, count), BF16))(
        partial, came, weights
    )
    return routed.T


def solution(mesh):
    placed = (
        P("expert", "group"),
        P("expert", None),
        P("expert", None),
        P("expert", None, None, "group"),
        P("expert", None, "group"),
    )
    return jax.shard_map(
        local, mesh=mesh, in_specs=placed, out_specs=P("expert", "group"), check_vma=False
    )
```

```python
import jax
import jax.numpy as jnp
from jax import lax
from jax.experimental import pallas as pl
from jax.experimental.pallas import tpu as pltpu
from jax.sharding import PartitionSpec as P

CAP = 18
HALF = 9
EXPERTS = 32
DEPTH = 8
PAIR = 2
WIDTH = 448
PADDED = 512
MAIN = EXPERTS * 8
ROWS = EXPERTS * HALF
SHARD = 39
F32 = jnp.float32
BF16 = jnp.bfloat16
NT = (((1,), (1,)), ((), ()))
TN = (((0,), (0,)), ((), ()))
VMEM_BYTES = 32 * 1024 * 1024


def row_of_eight(shape):
    return lax.broadcasted_iota(jnp.int32, shape, 0) & 7


def spread(count):
    row = lax.broadcasted_iota(jnp.int32, (8 * count, count), 0)
    column = lax.broadcasted_iota(jnp.int32, (8 * count, count), 1)
    return ((row >> 3) == column).astype(BF16)


def pack(main, last):
    row = row_of_eight((MAIN, 128))
    lane = lax.broadcasted_iota(jnp.int32, (MAIN, 128), 1)
    even = jnp.zeros((MAIN, 128), F32)
    odd = jnp.zeros((MAIN, 128), F32)
    for tile in range(4):
        piece = last[:, 128 * tile : 128 * tile + 128]
        even = jnp.where(row == 2 * tile, piece, even)
        odd = jnp.where(row == 2 * tile + 1, piece, odd)
    runs = odd + pltpu.roll(even, 64, 1)
    tail = jnp.where(lane < 64, main[:, 384:512], runs)
    tiles = [main[:, 128 * tile : 128 * tile + 128] for tile in range(3)] + [tail]
    return jnp.concatenate([t.reshape(EXPERTS, 8, 128) for t in tiles], axis=1).astype(BF16)


def opened(block):
    wide = block.astype(F32)
    tiles = [wide[:, 8 * tile : 8 * tile + 8, :].reshape(MAIN, 128) for tile in range(4)]
    row = row_of_eight((MAIN, 128))
    lane = lax.broadcasted_iota(jnp.int32, (MAIN, 128), 1)
    tail = tiles[3]
    main = jnp.concatenate(tiles[:3] + [jnp.where(lane < 64, tail, 0.0)], axis=1).astype(BF16)
    turned = pltpu.roll(tail, 64, 1)
    runs = [
        jnp.where(
            (row == 2 * tile) & (lane < 64),
            turned,
            jnp.where((row == 2 * tile + 1) & (lane >= 64), tail, 0.0),
        )
        for tile in range(4)
    ]
    return main, jnp.concatenate(runs, axis=1).astype(BF16)


def unpack(block):
    main, runs = opened(block)
    last = lax.dot_general(spread(EXPERTS), runs, TN, preferred_element_type=F32).astype(BF16)
    return jnp.concatenate([main, last], axis=0)


def eightfold(x):
    return jnp.broadcast_to(x[:, None, :], (x.shape[0], 8, x.shape[1])).reshape(8 * x.shape[0], x.shape[1])


def halves(rows, shift):
    index = lax.broadcasted_iota(jnp.int32, (rows, 1), 0)
    return ((index >> shift) & 1) * HALF


def labels(shape):
    index = lax.broadcasted_iota(jnp.int32, shape, 0)
    return (index & (EXPERTS - PAIR)) | (index >> 5)


def slots(ids_ref, label):
    count = ids_ref.shape[1]
    chosen = jnp.zeros(label.shape, F32)
    for pick in range(ids_ref.shape[0]):
        chosen = jnp.where(ids_ref[pick : pick + 1, :] == label, 1.0, chosen)
    before = lax.broadcasted_iota(jnp.int32, (count, count), 0) < lax.broadcasted_iota(
        jnp.int32, (count, count), 1
    )
    earlier = jnp.dot(chosen.astype(BF16), before.astype(BF16), preferred_element_type=F32)
    return jnp.where(chosen > 0.0, earlier, -1.0)


def dispatch_kernel(ids_hbm, tokens_hbm, send_ref, mark_ref, ids_ref, tokens_ref, ids_sem, tokens_sem):
    ids_copy = pltpu.make_async_copy(ids_hbm, ids_ref, ids_sem)
    tokens_copy = pltpu.make_async_copy(tokens_hbm, tokens_ref, tokens_sem)
    ids_copy.start()
    tokens_copy.start()
    count = ids_ref.shape[1]
    mark_ref[...] = jnp.zeros(mark_ref.shape, F32)
    ids_copy.wait()
    every = eightfold(slots(ids_ref, labels((PAIR * EXPERTS, count))))
    first = halves(every.shape[0], 3)
    place = (row_of_eight((every.shape[0], 1)) + first).astype(F32)
    tokens_copy.wait()
    tokens = jnp.concatenate(
        [tokens_ref[...], jnp.zeros((PADDED - WIDTH, count), BF16)], axis=0
    )
    main = (every == place).astype(BF16)
    last = (every == (first + 8).astype(F32)).astype(BF16)
    main = lax.dot_general(main, tokens, NT, preferred_element_type=F32)
    last = lax.dot_general(last, tokens, NT, preferred_element_type=F32)
    for chip in range(PAIR):
        rows = slice(MAIN * chip, MAIN * chip + MAIN)
        send_ref[EXPERTS * chip : EXPERTS * chip + EXPERTS] = pack(main[rows], last[rows])


def weights_kernel(core_ref, mark_ref, ids_ref, combine_ref, weights_ref):
    del mark_ref
    core = core_ref[0]
    index = lax.broadcasted_iota(jnp.int32, (PAIR * EXPERTS, ids_ref.shape[1]), 0)
    label = 2 * (index & 15) + ((index >> 4) & 1)
    slot = slots(ids_ref, label)
    weight = jnp.zeros(slot.shape, F32)
    for pick in range(ids_ref.shape[0]):
        weight = jnp.where(
            ids_ref[pick : pick + 1, :] == label, combine_ref[pick : pick + 1, :], weight
        )
    for part in range(PAIR):
        first = (HALF * (core if part == 0 else 1 - core)).astype(F32)
        own = slice(EXPERTS * part, EXPERTS * part + EXPERTS)
        every, each = eightfold(slot[own]), eightfold(weight[own])
        place = row_of_eight((MAIN, 1)).astype(F32) + first
        main = jnp.where(every == place, each, 0.0)
        last = jnp.where(slot[own] == first + 8.0, weight[own], 0.0)
        both = jnp.concatenate([main, last], axis=0)
        high = both.astype(BF16)
        low = (both - high.astype(F32)).astype(BF16)
        weights_ref[part] = jnp.concatenate([high, low], axis=1)


def ordered(count, blocks, column, last):
    per = count // blocks
    lasts = EXPERTS // blocks
    mains = lasts * 8
    row = lax.broadcasted_iota(jnp.int32, (count, MAIN), 0)
    block = lax.div(row, per)
    inside = row - block * per
    if last:
        chosen = (
            (inside >= mains)
            & (inside < mains + lasts)
            & ((column >> 3) == block * lasts + inside - mains)
        )
    else:
        chosen = (inside < mains) & (column == block * mains + inside)
    return chosen.astype(BF16)


def own_gate_up_kernel(core_ref, arrived_ref, own_hbm, partial_ref, rows_ref, own_ref, sems):
    copies = [
        pltpu.make_async_copy(own_hbm.at[index], own_ref.at[index], sems.at[index])
        for index in range(2)
    ]
    for copy in copies:
        copy.start()
    side = 1 - core_ref[0]
    column = lax.broadcasted_iota(jnp.int32, (SHARD * DEPTH, MAIN), 1)
    take_main = ordered(SHARD * DEPTH, DEPTH, column, False)
    take_last = ordered(SHARD * DEPTH, DEPTH, column, True)
    rows = []
    for which in (side, 1 - side):
        main, runs = opened(arrived_ref[pl.ds(which * EXPERTS, EXPERTS)])
        taken = jnp.dot(take_main, main, preferred_element_type=F32)
        taken += jnp.dot(take_last, runs, preferred_element_type=F32)
        rows.append(taken.astype(BF16))
    rows_ref[...] = rows[1]
    units = own_ref.shape[2]
    for index in range(2):
        copies[index].wait()
        for start in range(0, units, PADDED):
            part = jnp.dot(
                rows[0][:, :WIDTH],
                own_ref[index, :, start : start + PADDED],
                preferred_element_type=F32,
            )
            partial_ref[:, index * units + start : index * units + start + PADDED] = part


def other_gate_up_kernel(partial_ref, rows_ref, other_ref, terms_ref):
    units = other_ref.shape[2]
    for index in range(2):
        for start in range(0, units, PADDED):
            at = slice(index * units + start, index * units + start + PADDED)
            part = jnp.dot(
                rows_ref[:, :WIDTH],
                other_ref[index, :, start : start + PADDED],
                preferred_element_type=F32,
            )
            terms_ref[:, at] = (partial_ref[:, at] + part).astype(BF16)


def hidden_kernel(sums_ref, hidden_ref):
    units = sums_ref.shape[1] // 2
    count = sums_ref.shape[0]
    lasts = EXPERTS // DEPTH
    mains = lasts * 8
    both = sums_ref[...].astype(F32)
    gate, up = both[:, :units], both[:, units:]
    hidden = (gate / (1.0 + jnp.exp(-gate)) * up).astype(BF16)
    row = lax.broadcasted_iota(jnp.int32, (mains, count), 0)
    column = lax.broadcasted_iota(jnp.int32, (mains, count), 1)
    pick = (column == mains + lax.rem(row, lasts)).astype(BF16)
    again = jnp.dot(pick, hidden, preferred_element_type=F32)
    run = lax.div(lax.broadcasted_iota(jnp.int32, (mains, 128), 0), lasts)
    extra = jnp.zeros((mains, 128), F32)
    for tile in range(units // 128):
        extra = jnp.where(run == tile, again[:, 128 * tile : 128 * tile + 128], extra)
    block = jnp.concatenate([hidden[:mains], extra.astype(BF16)], axis=1)
    for piece in range(DEPTH):
        hidden_ref[piece] = block


def gathered_hidden(hidden_ref):
    mains = hidden_ref.shape[1]
    units = hidden_ref.shape[2] - 128
    lasts = EXPERTS // DEPTH
    main = jnp.concatenate([hidden_ref[piece, :, :units] for piece in range(DEPTH)], axis=0)
    extra = jnp.concatenate([hidden_ref[piece, :, units:] for piece in range(DEPTH)], axis=0)
    row = lax.broadcasted_iota(jnp.int32, extra.shape, 0)
    run = lax.div(lax.rem(row, mains), lasts)
    wide = extra.astype(F32)
    runs = jnp.concatenate(
        [jnp.where(run == tile, wide, 0.0) for tile in range(units // 128)], axis=1
    ).astype(BF16)
    source = lax.broadcasted_iota(jnp.int32, (EXPERTS, DEPTH * mains), 0)
    column = lax.broadcasted_iota(jnp.int32, (EXPERTS, DEPTH * mains), 1)
    pick = source == lax.div(column, mains) * lasts + lax.rem(column, lasts)
    last = jnp.dot(pick.astype(BF16), runs, preferred_element_type=F32).astype(BF16)
    return jnp.concatenate([main, last], axis=0)


def down_kernel(core_ref, hidden_ref, own_hbm, other_ref, send_ref, own_ref, sem):
    copy = pltpu.make_async_copy(own_hbm, own_ref, sem)
    copy.start()
    core = core_ref[0]
    hidden = gathered_hidden(hidden_ref)
    chips = EXPERTS // 2
    for ref, where in ((other_ref, core), (own_ref, 1 - core)):
        if ref is own_ref:
            copy.wait()
        down = jnp.concatenate(
            [ref[...], jnp.zeros((PADDED - WIDTH, ref.shape[1]), BF16)], axis=0
        )
        result = lax.dot_general(hidden, down, NT, preferred_element_type=F32).astype(BF16)
        last = jnp.dot(spread(EXPERTS), result[MAIN:], preferred_element_type=F32)
        blocks = pack(result[:MAIN].astype(F32), last).reshape(chips, 2, 32, 128)
        at = pl.ds(where * chips, chips)
        send_ref[at, pl.ds(core, 1)] = blocks[:, 0:1]
        send_ref[at, pl.ds(1 - core, 1)] = blocks[:, 1:2]


def kept_kernel(back_ref, weights_ref, partial_ref):
    partial_ref[...] = lax.dot_general(
        unpack(back_ref[:, 0]), weights_ref[0], TN, preferred_element_type=F32
    )[:WIDTH]


def combine_kernel(partial_ref, came_ref, weights_ref, out_ref):
    routed = partial_ref[...]
    routed += lax.dot_general(
        unpack(came_ref[...]), weights_ref[1], TN, preferred_element_type=F32
    )[:WIDTH]
    count = out_ref.shape[1]
    out_ref[...] = (routed[:, :count] + routed[:, count:]).astype(BF16)


def call(kernel, out, **more):
    return pl.pallas_call(
        kernel,
        out_shape=out,
        compiler_params=pltpu.CompilerParams(vmem_limit_bytes=VMEM_BYTES),
        **more,
    )


def local(tokens, expert_ids, combine, w_in, w_down):
    count = tokens.shape[0]
    hidden_units = w_down.shape[1]
    core = (lax.axis_index("expert") & 1).astype(jnp.int32).reshape(1)
    everyone = ("group", "expert")
    along_z = [[x * DEPTH + z for z in range(DEPTH)] for x in range(PAIR)]
    along_plane = [
        [(x * DEPTH + z) * EXPERTS + e for x in range(PAIR) for e in range(EXPERTS)]
        for z in range(DEPTH)
    ]
    along_core = [
        [(x * DEPTH + z) * EXPERTS + 2 * y + c for x in range(PAIR) for y in range(EXPERTS // 2)]
        for z in range(DEPTH)
        for c in range(2)
    ]
    turn = [
        ((x * DEPTH + z) * EXPERTS + 2 * y + c, (c * DEPTH + z) * EXPERTS + 2 * y + 1 - x)
        for x in range(PAIR)
        for z in range(DEPTH)
        for y in range(EXPERTS // 2)
        for c in range(2)
    ]
    cores = [(e, e ^ 1) for e in range(EXPERTS)]
    tokens, ids, combine = tokens.T, expert_ids.T, combine.T
    w_in = jnp.swapaxes(w_in[0], 1, 2)
    w_down = w_down[0].T
    scalar = pl.BlockSpec(memory_space=pltpu.SMEM)
    whole = pl.BlockSpec(memory_space=pltpu.VMEM)
    anywhere = pl.BlockSpec(memory_space=pl.ANY)
    packed = (PAIR * EXPERTS, 32, 128)

    own_in = lax.ppermute(w_in, everyone, turn)
    send, mark = call(
        dispatch_kernel,
        (jax.ShapeDtypeStruct(packed, BF16), jax.ShapeDtypeStruct((8, 128), F32)),
        in_specs=[pl.BlockSpec(memory_space=pltpu.HBM)] * 2,
        scratch_shapes=[
            pltpu.VMEM(ids.shape, jnp.int32),
            pltpu.VMEM(tokens.shape, BF16),
            pltpu.SemaphoreType.DMA,
            pltpu.SemaphoreType.DMA,
        ],
    )(
        pltpu.with_memory_space_constraint(ids, pltpu.HBM),
        pltpu.with_memory_space_constraint(tokens, pltpu.HBM),
    )
    arrived = lax.all_to_all(
        send, everyone, 0, 0, axis_index_groups=along_plane, tiled=True
    )
    own_in, w_down, mark = lax.optimization_barrier((own_in, w_down, mark))
    other_in = lax.ppermute(own_in, "expert", cores)
    own_down = lax.ppermute(w_down, everyone, turn)
    partial, rows = call(
        own_gate_up_kernel,
        (
            jax.ShapeDtypeStruct((SHARD * DEPTH, 2 * hidden_units), F32),
            jax.ShapeDtypeStruct((SHARD * DEPTH, PADDED), BF16),
        ),
        in_specs=[scalar, whole, anywhere],
        scratch_shapes=[pltpu.VMEM(own_in.shape, BF16), pltpu.SemaphoreType.DMA((2,))],
        cost_estimate=pl.CostEstimate(
            flops=50 * 10**9, bytes_accessed=4 * 1024 * 1024, transcendentals=0
        ),
    )(core, arrived, pltpu.with_memory_space_constraint(own_in, pltpu.HBM))
    terms = call(
        other_gate_up_kernel, jax.ShapeDtypeStruct((SHARD * DEPTH, 2 * hidden_units), BF16)
    )(partial, rows, other_in)
    sums = lax.psum_scatter(
        terms, "group", scatter_dimension=0, axis_index_groups=along_z, tiled=True
    )
    sums, own_down = lax.optimization_barrier((sums, own_down))
    other_down = lax.ppermute(own_down, "expert", cores)
    mains = EXPERTS // DEPTH * 8
    hidden = call(
        hidden_kernel, jax.ShapeDtypeStruct((DEPTH, mains, hidden_units + 128), BF16)
    )(sums)
    hidden = lax.all_to_all(hidden, "group", 0, 0, axis_index_groups=along_z, tiled=True)
    send = call(
        down_kernel,
        jax.ShapeDtypeStruct((EXPERTS, 2, 32, 128), BF16),
        in_specs=[scalar, whole, anywhere, whole],
        scratch_shapes=[pltpu.VMEM(own_down.shape, BF16), pltpu.SemaphoreType.DMA],
    )(core, hidden, pltpu.with_memory_space_constraint(own_down, pltpu.HBM), other_down)
    back = lax.all_to_all(send, everyone, 0, 0, axis_index_groups=along_core, tiled=True)
    came = lax.ppermute(back[:, 1], "expert", cores)
    weights = call(
        weights_kernel,
        jax.ShapeDtypeStruct((PAIR, ROWS, 2 * count), BF16),
        in_specs=[scalar, whole, whole, whole],
    )(core, mark, ids, combine)
    partial = call(kept_kernel, jax.ShapeDtypeStruct((WIDTH, 2 * count), F32))(back, weights)
    routed = call(combine_kernel, jax.ShapeDtypeStruct((WIDTH, count), BF16))(
        partial, came, weights
    )
    return routed.T


def solution(mesh):
    placed = (
        P("expert", "group"),
        P("expert", None),
        P("expert", None),
        P("expert", None, None, "group"),
        P("expert", None, "group"),
    )
    return jax.shard_map(
        local, mesh=mesh, in_specs=placed, out_specs=P("expert", "group"), check_vma=False
    )
```

```python
import jax
import jax.numpy as jnp
from jax import lax
from jax.experimental import pallas as pl
from jax.experimental.pallas import tpu as pltpu
from jax.sharding import PartitionSpec as P

CAP = 18
HALF = 9
EXPERTS = 32
DEPTH = 8
PAIR = 2
WIDTH = 448
PADDED = 512
MAIN = EXPERTS * 8
ROWS = EXPERTS * HALF
SHARD = 39
F32 = jnp.float32
BF16 = jnp.bfloat16
NT = (((1,), (1,)), ((), ()))
TN = (((0,), (0,)), ((), ()))
VMEM_BYTES = 32 * 1024 * 1024


def row_of_eight(shape):
    return lax.broadcasted_iota(jnp.int32, shape, 0) & 7


def spread(count):
    row = lax.broadcasted_iota(jnp.int32, (8 * count, count), 0)
    column = lax.broadcasted_iota(jnp.int32, (8 * count, count), 1)
    return ((row >> 3) == column).astype(BF16)


def pack(main, last):
    row = row_of_eight((MAIN, 128))
    lane = lax.broadcasted_iota(jnp.int32, (MAIN, 128), 1)
    even = jnp.zeros((MAIN, 128), F32)
    odd = jnp.zeros((MAIN, 128), F32)
    for tile in range(4):
        piece = last[:, 128 * tile : 128 * tile + 128]
        even = jnp.where(row == 2 * tile, piece, even)
        odd = jnp.where(row == 2 * tile + 1, piece, odd)
    runs = odd + pltpu.roll(even, 64, 1)
    tail = jnp.where(lane < 64, main[:, 384:512], runs)
    tiles = [main[:, 128 * tile : 128 * tile + 128] for tile in range(3)] + [tail]
    return jnp.concatenate([t.reshape(EXPERTS, 8, 128) for t in tiles], axis=1).astype(BF16)


def opened(block):
    wide = block.astype(F32)
    tiles = [wide[:, 8 * tile : 8 * tile + 8, :].reshape(MAIN, 128) for tile in range(4)]
    row = row_of_eight((MAIN, 128))
    lane = lax.broadcasted_iota(jnp.int32, (MAIN, 128), 1)
    tail = tiles[3]
    main = jnp.concatenate(tiles[:3] + [jnp.where(lane < 64, tail, 0.0)], axis=1).astype(BF16)
    turned = pltpu.roll(tail, 64, 1)
    runs = [
        jnp.where(
            (row == 2 * tile) & (lane < 64),
            turned,
            jnp.where((row == 2 * tile + 1) & (lane >= 64), tail, 0.0),
        )
        for tile in range(4)
    ]
    return main, jnp.concatenate(runs, axis=1).astype(BF16)


def unpack(block):
    main, runs = opened(block)
    last = lax.dot_general(spread(EXPERTS), runs, TN, preferred_element_type=F32).astype(BF16)
    return jnp.concatenate([main, last], axis=0)


def eightfold(x):
    return jnp.broadcast_to(x[:, None, :], (x.shape[0], 8, x.shape[1])).reshape(8 * x.shape[0], x.shape[1])


def halves(rows, shift):
    index = lax.broadcasted_iota(jnp.int32, (rows, 1), 0)
    return ((index >> shift) & 1) * HALF


def labels(shape):
    index = lax.broadcasted_iota(jnp.int32, shape, 0)
    return (index & (EXPERTS - PAIR)) | (index >> 5)


def slots(ids_ref, label):
    count = ids_ref.shape[1]
    chosen = jnp.zeros(label.shape, F32)
    for pick in range(ids_ref.shape[0]):
        chosen = jnp.where(ids_ref[pick : pick + 1, :] == label, 1.0, chosen)
    before = lax.broadcasted_iota(jnp.int32, (count, count), 0) < lax.broadcasted_iota(
        jnp.int32, (count, count), 1
    )
    earlier = jnp.dot(chosen.astype(BF16), before.astype(BF16), preferred_element_type=F32)
    return jnp.where(chosen > 0.0, earlier, -1.0)


def dispatch_kernel(ids_hbm, tokens_hbm, send_ref, mark_ref, ids_ref, tokens_ref, ids_sem, tokens_sem):
    ids_copy = pltpu.make_async_copy(ids_hbm, ids_ref, ids_sem)
    tokens_copy = pltpu.make_async_copy(tokens_hbm, tokens_ref, tokens_sem)
    ids_copy.start()
    tokens_copy.start()
    count = ids_ref.shape[1]
    mark_ref[...] = jnp.zeros(mark_ref.shape, F32)
    ids_copy.wait()
    every = eightfold(slots(ids_ref, labels((PAIR * EXPERTS, count))))
    first = halves(every.shape[0], 3)
    place = (row_of_eight((every.shape[0], 1)) + first).astype(F32)
    tokens_copy.wait()
    tokens = jnp.concatenate(
        [tokens_ref[...], jnp.zeros((PADDED - WIDTH, count), BF16)], axis=0
    )
    main = (every == place).astype(BF16)
    last = (every == (first + 8).astype(F32)).astype(BF16)
    main = lax.dot_general(main, tokens, NT, preferred_element_type=F32)
    last = lax.dot_general(last, tokens, NT, preferred_element_type=F32)
    for chip in range(PAIR):
        rows = slice(MAIN * chip, MAIN * chip + MAIN)
        send_ref[EXPERTS * chip : EXPERTS * chip + EXPERTS] = pack(main[rows], last[rows])


def weights_kernel(core_ref, mark_ref, ids_ref, combine_ref, weights_ref):
    del mark_ref
    core = core_ref[0]
    index = lax.broadcasted_iota(jnp.int32, (PAIR * EXPERTS, ids_ref.shape[1]), 0)
    label = 2 * (index & 15) + ((index >> 4) & 1)
    slot = slots(ids_ref, label)
    weight = jnp.zeros(slot.shape, F32)
    for pick in range(ids_ref.shape[0]):
        weight = jnp.where(
            ids_ref[pick : pick + 1, :] == label, combine_ref[pick : pick + 1, :], weight
        )
    for part in range(PAIR):
        first = (HALF * (core if part == 0 else 1 - core)).astype(F32)
        own = slice(EXPERTS * part, EXPERTS * part + EXPERTS)
        every, each = eightfold(slot[own]), eightfold(weight[own])
        place = row_of_eight((MAIN, 1)).astype(F32) + first
        main = jnp.where(every == place, each, 0.0)
        last = jnp.where(slot[own] == first + 8.0, weight[own], 0.0)
        both = jnp.concatenate([main, last], axis=0)
        high = both.astype(BF16)
        low = (both - high.astype(F32)).astype(BF16)
        weights_ref[part] = jnp.concatenate([high, low], axis=1)


def ordered(count, blocks, column, last):
    per = count // blocks
    lasts = EXPERTS // blocks
    mains = lasts * 8
    row = lax.broadcasted_iota(jnp.int32, (count, MAIN), 0)
    block = lax.div(row, per)
    inside = row - block * per
    if last:
        chosen = (
            (inside >= mains)
            & (inside < mains + lasts)
            & ((column >> 3) == block * lasts + inside - mains)
        )
    else:
        chosen = (inside < mains) & (column == block * mains + inside)
    return chosen.astype(BF16)


def own_gate_up_kernel(core_ref, arrived_ref, own_hbm, partial_ref, rows_ref, own_ref, sems):
    copies = [
        pltpu.make_async_copy(own_hbm.at[index], own_ref.at[index], sems.at[index])
        for index in range(2)
    ]
    for copy in copies:
        copy.start()
    side = 1 - core_ref[0]
    column = lax.broadcasted_iota(jnp.int32, (SHARD * DEPTH, MAIN), 1)
    take_main = ordered(SHARD * DEPTH, DEPTH, column, False)
    take_last = ordered(SHARD * DEPTH, DEPTH, column, True)
    rows = []
    for which in (side, 1 - side):
        main, runs = opened(arrived_ref[pl.ds(which * EXPERTS, EXPERTS)])
        taken = jnp.dot(take_main, main, preferred_element_type=F32)
        taken += jnp.dot(take_last, runs, preferred_element_type=F32)
        rows.append(taken.astype(BF16))
    rows_ref[...] = rows[1]
    units = own_ref.shape[2]
    for index in range(2):
        copies[index].wait()
        for start in range(0, units, PADDED):
            part = jnp.dot(
                rows[0][:, :WIDTH],
                own_ref[index, :, start : start + PADDED],
                preferred_element_type=F32,
            )
            partial_ref[:, index * units + start : index * units + start + PADDED] = part


def other_gate_up_kernel(partial_ref, rows_ref, other_ref, terms_ref):
    units = other_ref.shape[2]
    for index in range(2):
        for start in range(0, units, PADDED):
            at = slice(index * units + start, index * units + start + PADDED)
            part = jnp.dot(
                rows_ref[:, :WIDTH],
                other_ref[index, :, start : start + PADDED],
                preferred_element_type=F32,
            )
            terms_ref[:, at] = (partial_ref[:, at] + part).astype(BF16)


def hidden_kernel(sums_ref, hidden_ref):
    units = sums_ref.shape[1] // 2
    count = sums_ref.shape[0]
    lasts = EXPERTS // DEPTH
    mains = lasts * 8
    both = sums_ref[...].astype(F32)
    gate, up = both[:, :units], both[:, units:]
    hidden = (gate / (1.0 + jnp.exp(-gate)) * up).astype(BF16)
    row = lax.broadcasted_iota(jnp.int32, (mains, count), 0)
    column = lax.broadcasted_iota(jnp.int32, (mains, count), 1)
    pick = (column == mains + lax.rem(row, lasts)).astype(BF16)
    again = jnp.dot(pick, hidden, preferred_element_type=F32)
    run = lax.div(lax.broadcasted_iota(jnp.int32, (mains, 128), 0), lasts)
    extra = jnp.zeros((mains, 128), F32)
    for tile in range(units // 128):
        extra = jnp.where(run == tile, again[:, 128 * tile : 128 * tile + 128], extra)
    block = jnp.concatenate([hidden[:mains], extra.astype(BF16)], axis=1)
    for piece in range(DEPTH):
        hidden_ref[piece] = block


def gathered_hidden(hidden_ref):
    mains = hidden_ref.shape[1]
    units = hidden_ref.shape[2] - 128
    lasts = EXPERTS // DEPTH
    main = jnp.concatenate([hidden_ref[piece, :, :units] for piece in range(DEPTH)], axis=0)
    extra = jnp.concatenate([hidden_ref[piece, :, units:] for piece in range(DEPTH)], axis=0)
    row = lax.broadcasted_iota(jnp.int32, extra.shape, 0)
    run = lax.div(lax.rem(row, mains), lasts)
    wide = extra.astype(F32)
    runs = jnp.concatenate(
        [jnp.where(run == tile, wide, 0.0) for tile in range(units // 128)], axis=1
    ).astype(BF16)
    source = lax.broadcasted_iota(jnp.int32, (EXPERTS, DEPTH * mains), 0)
    column = lax.broadcasted_iota(jnp.int32, (EXPERTS, DEPTH * mains), 1)
    pick = source == lax.div(column, mains) * lasts + lax.rem(column, lasts)
    last = jnp.dot(pick.astype(BF16), runs, preferred_element_type=F32).astype(BF16)
    return jnp.concatenate([main, last], axis=0)


def down_kernel(core_ref, hidden_ref, own_hbm, other_ref, send_ref, own_ref, sem):
    copy = pltpu.make_async_copy(own_hbm, own_ref, sem)
    copy.start()
    core = core_ref[0]
    hidden = gathered_hidden(hidden_ref)
    chips = EXPERTS // 2
    for ref, where in ((other_ref, core), (own_ref, 1 - core)):
        if ref is own_ref:
            copy.wait()
        down = jnp.concatenate(
            [ref[...], jnp.zeros((PADDED - WIDTH, ref.shape[1]), BF16)], axis=0
        )
        result = lax.dot_general(hidden, down, NT, preferred_element_type=F32).astype(BF16)
        last = jnp.dot(spread(EXPERTS), result[MAIN:], preferred_element_type=F32)
        blocks = pack(result[:MAIN].astype(F32), last).reshape(chips, 2, 32, 128)
        at = pl.ds(where * chips, chips)
        send_ref[at, pl.ds(core, 1)] = blocks[:, 0:1]
        send_ref[at, pl.ds(1 - core, 1)] = blocks[:, 1:2]


def kept_kernel(back_ref, weights_ref, partial_ref):
    partial_ref[...] = lax.dot_general(
        unpack(back_ref[:, 0]), weights_ref[0], TN, preferred_element_type=F32
    )[:WIDTH]


def combine_kernel(partial_ref, came_ref, weights_ref, out_ref):
    routed = partial_ref[...]
    routed += lax.dot_general(
        unpack(came_ref[...]), weights_ref[1], TN, preferred_element_type=F32
    )[:WIDTH]
    count = out_ref.shape[1]
    out_ref[...] = (routed[:, :count] + routed[:, count:]).astype(BF16)


def call(kernel, out, **more):
    return pl.pallas_call(
        kernel,
        out_shape=out,
        compiler_params=pltpu.CompilerParams(vmem_limit_bytes=VMEM_BYTES),
        **more,
    )


def local(tokens, expert_ids, combine, w_in, w_down):
    count = tokens.shape[0]
    hidden_units = w_down.shape[1]
    core = (lax.axis_index("expert") & 1).astype(jnp.int32).reshape(1)
    everyone = ("group", "expert")
    along_z = [[x * DEPTH + z for z in range(DEPTH)] for x in range(PAIR)]
    along_plane = [
        [(x * DEPTH + z) * EXPERTS + e for x in range(PAIR) for e in range(EXPERTS)]
        for z in range(DEPTH)
    ]
    along_core = [
        [(x * DEPTH + z) * EXPERTS + 2 * y + c for x in range(PAIR) for y in range(EXPERTS // 2)]
        for z in range(DEPTH)
        for c in range(2)
    ]
    turn = [
        ((x * DEPTH + z) * EXPERTS + 2 * y + c, (c * DEPTH + z) * EXPERTS + 2 * y + 1 - x)
        for x in range(PAIR)
        for z in range(DEPTH)
        for y in range(EXPERTS // 2)
        for c in range(2)
    ]
    cores = [(e, e ^ 1) for e in range(EXPERTS)]
    tokens, ids, combine = tokens.T, expert_ids.T, combine.T
    w_in = jnp.swapaxes(w_in[0], 1, 2)
    w_down = w_down[0].T
    scalar = pl.BlockSpec(memory_space=pltpu.SMEM)
    whole = pl.BlockSpec(memory_space=pltpu.VMEM)
    anywhere = pl.BlockSpec(memory_space=pl.ANY)
    packed = (PAIR * EXPERTS, 32, 128)

    own_in = lax.ppermute(w_in, everyone, turn)
    send, mark = call(
        dispatch_kernel,
        (jax.ShapeDtypeStruct(packed, BF16), jax.ShapeDtypeStruct((8, 128), F32)),
        in_specs=[pl.BlockSpec(memory_space=pltpu.HBM)] * 2,
        scratch_shapes=[
            pltpu.VMEM(ids.shape, jnp.int32),
            pltpu.VMEM(tokens.shape, BF16),
            pltpu.SemaphoreType.DMA,
            pltpu.SemaphoreType.DMA,
        ],
    )(
        pltpu.with_memory_space_constraint(ids, pltpu.HBM),
        pltpu.with_memory_space_constraint(tokens, pltpu.HBM),
    )
    arrived = lax.all_to_all(
        send, everyone, 0, 0, axis_index_groups=along_plane, tiled=True
    )
    w_down, mark = lax.optimization_barrier((w_down, mark))
    own_in, mark = lax.optimization_barrier((own_in, mark))
    other_in = lax.ppermute(own_in, "expert", cores)
    own_down = lax.ppermute(w_down, everyone, turn)
    partial, rows = call(
        own_gate_up_kernel,
        (
            jax.ShapeDtypeStruct((SHARD * DEPTH, 2 * hidden_units), F32),
            jax.ShapeDtypeStruct((SHARD * DEPTH, PADDED), BF16),
        ),
        in_specs=[scalar, whole, anywhere],
        scratch_shapes=[pltpu.VMEM(own_in.shape, BF16), pltpu.SemaphoreType.DMA((2,))],
        cost_estimate=pl.CostEstimate(
            flops=50 * 10**9, bytes_accessed=4 * 1024 * 1024, transcendentals=0
        ),
    )(core, arrived, pltpu.with_memory_space_constraint(own_in, pltpu.HBM))
    terms = call(
        other_gate_up_kernel, jax.ShapeDtypeStruct((SHARD * DEPTH, 2 * hidden_units), BF16)
    )(partial, rows, other_in)
    sums = lax.psum_scatter(
        terms, "group", scatter_dimension=0, axis_index_groups=along_z, tiled=True
    )
    sums, own_down = lax.optimization_barrier((sums, own_down))
    other_down = lax.ppermute(own_down, "expert", cores)
    mains = EXPERTS // DEPTH * 8
    hidden = call(
        hidden_kernel, jax.ShapeDtypeStruct((DEPTH, mains, hidden_units + 128), BF16)
    )(sums)
    hidden = lax.all_to_all(hidden, "group", 0, 0, axis_index_groups=along_z, tiled=True)
    weights = call(
        weights_kernel,
        jax.ShapeDtypeStruct((PAIR, ROWS, 2 * count), BF16),
        in_specs=[scalar, whole, whole, whole],
    )(core, mark, ids, combine)
    hidden, weights = lax.optimization_barrier((hidden, weights))
    send = call(
        down_kernel,
        jax.ShapeDtypeStruct((EXPERTS, 2, 32, 128), BF16),
        in_specs=[scalar, whole, anywhere, whole],
        scratch_shapes=[pltpu.VMEM(own_down.shape, BF16), pltpu.SemaphoreType.DMA],
    )(core, hidden, pltpu.with_memory_space_constraint(own_down, pltpu.HBM), other_down)
    back = lax.all_to_all(send, everyone, 0, 0, axis_index_groups=along_core, tiled=True)
    came = lax.ppermute(back[:, 1], "expert", cores)
    partial = call(kept_kernel, jax.ShapeDtypeStruct((WIDTH, 2 * count), F32))(back, weights)
    routed = call(combine_kernel, jax.ShapeDtypeStruct((WIDTH, count), BF16))(
        partial, came, weights
    )
    return routed.T


def solution(mesh):
    placed = (
        P("expert", "group"),
        P("expert", None),
        P("expert", None),
        P("expert", None, None, "group"),
        P("expert", None, "group"),
    )
    return jax.shard_map(
        local, mesh=mesh, in_specs=placed, out_specs=P("expert", "group"), check_vma=False
    )
```

```python
import jax
import jax.numpy as jnp
from jax import lax
from jax.experimental import pallas as pl
from jax.experimental.pallas import tpu as pltpu
from jax.sharding import PartitionSpec as P

CAP = 18
HALF = 9
EXPERTS = 32
DEPTH = 8
PAIR = 2
WIDTH = 448
PADDED = 512
MAIN = EXPERTS * 8
ROWS = EXPERTS * HALF
SHARD = 39
F32 = jnp.float32
BF16 = jnp.bfloat16
NT = (((1,), (1,)), ((), ()))
TN = (((0,), (0,)), ((), ()))
VMEM_BYTES = 32 * 1024 * 1024


def row_of_eight(shape):
    return lax.broadcasted_iota(jnp.int32, shape, 0) & 7


def spread(count):
    row = lax.broadcasted_iota(jnp.int32, (8 * count, count), 0)
    column = lax.broadcasted_iota(jnp.int32, (8 * count, count), 1)
    return ((row >> 3) == column).astype(BF16)


def pack(main, last):
    row = row_of_eight((MAIN, 128))
    lane = lax.broadcasted_iota(jnp.int32, (MAIN, 128), 1)
    even = jnp.zeros((MAIN, 128), F32)
    odd = jnp.zeros((MAIN, 128), F32)
    for tile in range(4):
        piece = last[:, 128 * tile : 128 * tile + 128]
        even = jnp.where(row == 2 * tile, piece, even)
        odd = jnp.where(row == 2 * tile + 1, piece, odd)
    runs = odd + pltpu.roll(even, 64, 1)
    tail = jnp.where(lane < 64, main[:, 384:512], runs)
    tiles = [main[:, 128 * tile : 128 * tile + 128] for tile in range(3)] + [tail]
    return jnp.concatenate([t.reshape(EXPERTS, 8, 128) for t in tiles], axis=1).astype(BF16)


def opened(block):
    wide = block.astype(F32)
    tiles = [wide[:, 8 * tile : 8 * tile + 8, :].reshape(MAIN, 128) for tile in range(4)]
    row = row_of_eight((MAIN, 128))
    lane = lax.broadcasted_iota(jnp.int32, (MAIN, 128), 1)
    tail = tiles[3]
    main = jnp.concatenate(tiles[:3] + [jnp.where(lane < 64, tail, 0.0)], axis=1).astype(BF16)
    turned = pltpu.roll(tail, 64, 1)
    runs = [
        jnp.where(
            (row == 2 * tile) & (lane < 64),
            turned,
            jnp.where((row == 2 * tile + 1) & (lane >= 64), tail, 0.0),
        )
        for tile in range(4)
    ]
    return main, jnp.concatenate(runs, axis=1).astype(BF16)


def unpack(block):
    main, runs = opened(block)
    last = lax.dot_general(spread(EXPERTS), runs, TN, preferred_element_type=F32).astype(BF16)
    return jnp.concatenate([main, last], axis=0)


def eightfold(x):
    return jnp.broadcast_to(x[:, None, :], (x.shape[0], 8, x.shape[1])).reshape(8 * x.shape[0], x.shape[1])


def halves(rows, shift):
    index = lax.broadcasted_iota(jnp.int32, (rows, 1), 0)
    return ((index >> shift) & 1) * HALF


def labels(shape):
    index = lax.broadcasted_iota(jnp.int32, shape, 0)
    return (index & (EXPERTS - PAIR)) | (index >> 5)


def slots(ids_ref, label):
    count = ids_ref.shape[1]
    chosen = jnp.zeros(label.shape, F32)
    for pick in range(ids_ref.shape[0]):
        chosen = jnp.where(ids_ref[pick : pick + 1, :] == label, 1.0, chosen)
    before = lax.broadcasted_iota(jnp.int32, (count, count), 0) < lax.broadcasted_iota(
        jnp.int32, (count, count), 1
    )
    earlier = jnp.dot(chosen.astype(BF16), before.astype(BF16), preferred_element_type=F32)
    return jnp.where(chosen > 0.0, earlier, -1.0)


def dispatch_kernel(ids_hbm, tokens_hbm, send_ref, mark_ref, ids_ref, tokens_ref, ids_sem, tokens_sem):
    ids_copy = pltpu.make_async_copy(ids_hbm, ids_ref, ids_sem)
    tokens_copy = pltpu.make_async_copy(tokens_hbm, tokens_ref, tokens_sem)
    ids_copy.start()
    tokens_copy.start()
    count = ids_ref.shape[1]
    mark_ref[...] = jnp.zeros(mark_ref.shape, F32)
    ids_copy.wait()
    every = eightfold(slots(ids_ref, labels((PAIR * EXPERTS, count))))
    first = halves(every.shape[0], 3)
    place = (row_of_eight((every.shape[0], 1)) + first).astype(F32)
    tokens_copy.wait()
    tokens = jnp.concatenate(
        [tokens_ref[...], jnp.zeros((PADDED - WIDTH, count), BF16)], axis=0
    )
    main = (every == place).astype(BF16)
    last = (every == (first + 8).astype(F32)).astype(BF16)
    main = lax.dot_general(main, tokens, NT, preferred_element_type=F32)
    last = lax.dot_general(last, tokens, NT, preferred_element_type=F32)
    for chip in range(PAIR):
        rows = slice(MAIN * chip, MAIN * chip + MAIN)
        send_ref[EXPERTS * chip : EXPERTS * chip + EXPERTS] = pack(main[rows], last[rows])


def weights_kernel(core_ref, mark_ref, ids_ref, combine_ref, down_ref, weights_ref, padded_ref):
    del mark_ref
    padded_ref[:WIDTH] = down_ref[...]
    padded_ref[WIDTH:] = jnp.zeros((PADDED - WIDTH, down_ref.shape[1]), BF16)
    core = core_ref[0]
    index = lax.broadcasted_iota(jnp.int32, (PAIR * EXPERTS, ids_ref.shape[1]), 0)
    label = 2 * (index & 15) + ((index >> 4) & 1)
    slot = slots(ids_ref, label)
    weight = jnp.zeros(slot.shape, F32)
    for pick in range(ids_ref.shape[0]):
        weight = jnp.where(
            ids_ref[pick : pick + 1, :] == label, combine_ref[pick : pick + 1, :], weight
        )
    for part in range(PAIR):
        first = (HALF * (core if part == 0 else 1 - core)).astype(F32)
        own = slice(EXPERTS * part, EXPERTS * part + EXPERTS)
        every, each = eightfold(slot[own]), eightfold(weight[own])
        place = row_of_eight((MAIN, 1)).astype(F32) + first
        main = jnp.where(every == place, each, 0.0)
        last = jnp.where(slot[own] == first + 8.0, weight[own], 0.0)
        both = jnp.concatenate([main, last], axis=0)
        high = both.astype(BF16)
        low = (both - high.astype(F32)).astype(BF16)
        weights_ref[part] = jnp.concatenate([high, low], axis=1)


def ordered(count, blocks, column, last):
    per = count // blocks
    lasts = EXPERTS // blocks
    mains = lasts * 8
    row = lax.broadcasted_iota(jnp.int32, (count, MAIN), 0)
    block = lax.div(row, per)
    inside = row - block * per
    if last:
        chosen = (
            (inside >= mains)
            & (inside < mains + lasts)
            & ((column >> 3) == block * lasts + inside - mains)
        )
    else:
        chosen = (inside < mains) & (column == block * mains + inside)
    return chosen.astype(BF16)


def own_gate_up_kernel(core_ref, arrived_ref, own_hbm, partial_ref, rows_ref, own_ref, sems):
    copies = [
        pltpu.make_async_copy(own_hbm.at[index], own_ref.at[index], sems.at[index])
        for index in range(2)
    ]
    for copy in copies:
        copy.start()
    side = 1 - core_ref[0]
    column = lax.broadcasted_iota(jnp.int32, (SHARD * DEPTH, MAIN), 1)
    take_main = ordered(SHARD * DEPTH, DEPTH, column, False)
    take_last = ordered(SHARD * DEPTH, DEPTH, column, True)
    rows = []
    for which in (side, 1 - side):
        main, runs = opened(arrived_ref[pl.ds(which * EXPERTS, EXPERTS)])
        taken = jnp.dot(take_main, main, preferred_element_type=F32)
        taken += jnp.dot(take_last, runs, preferred_element_type=F32)
        rows.append(taken.astype(BF16))
    rows_ref[...] = rows[1]
    units = own_ref.shape[2]
    for index in range(2):
        copies[index].wait()
        for start in range(0, units, PADDED):
            part = jnp.dot(
                rows[0][:, :WIDTH],
                own_ref[index, :, start : start + PADDED],
                preferred_element_type=F32,
            )
            partial_ref[:, index * units + start : index * units + start + PADDED] = part


def other_gate_up_kernel(partial_ref, rows_ref, other_ref, terms_ref):
    units = other_ref.shape[2]
    for index in range(2):
        for start in range(0, units, PADDED):
            at = slice(index * units + start, index * units + start + PADDED)
            part = jnp.dot(
                rows_ref[:, :WIDTH],
                other_ref[index, :, start : start + PADDED],
                preferred_element_type=F32,
            )
            terms_ref[:, at] = (partial_ref[:, at] + part).astype(BF16)


def hidden_kernel(sums_ref, hidden_ref):
    units = sums_ref.shape[1] // 2
    count = sums_ref.shape[0]
    lasts = EXPERTS // DEPTH
    mains = lasts * 8
    both = sums_ref[...].astype(F32)
    gate, up = both[:, :units], both[:, units:]
    hidden = (gate / (1.0 + jnp.exp(-gate)) * up).astype(BF16)
    row = lax.broadcasted_iota(jnp.int32, (mains, count), 0)
    column = lax.broadcasted_iota(jnp.int32, (mains, count), 1)
    pick = (column == mains + lax.rem(row, lasts)).astype(BF16)
    again = jnp.dot(pick, hidden, preferred_element_type=F32)
    run = lax.div(lax.broadcasted_iota(jnp.int32, (mains, 128), 0), lasts)
    extra = jnp.zeros((mains, 128), F32)
    for tile in range(units // 128):
        extra = jnp.where(run == tile, again[:, 128 * tile : 128 * tile + 128], extra)
    block = jnp.concatenate([hidden[:mains], extra.astype(BF16)], axis=1)
    for piece in range(DEPTH):
        hidden_ref[piece] = block


def gathered_hidden(hidden_ref):
    mains = hidden_ref.shape[1]
    units = hidden_ref.shape[2] - 128
    lasts = EXPERTS // DEPTH
    main = jnp.concatenate([hidden_ref[piece, :, :units] for piece in range(DEPTH)], axis=0)
    extra = jnp.concatenate([hidden_ref[piece, :, units:] for piece in range(DEPTH)], axis=0)
    row = lax.broadcasted_iota(jnp.int32, extra.shape, 0)
    run = lax.div(lax.rem(row, mains), lasts)
    wide = extra.astype(F32)
    runs = jnp.concatenate(
        [jnp.where(run == tile, wide, 0.0) for tile in range(units // 128)], axis=1
    ).astype(BF16)
    source = lax.broadcasted_iota(jnp.int32, (EXPERTS, DEPTH * mains), 0)
    column = lax.broadcasted_iota(jnp.int32, (EXPERTS, DEPTH * mains), 1)
    pick = source == lax.div(column, mains) * lasts + lax.rem(column, lasts)
    last = jnp.dot(pick.astype(BF16), runs, preferred_element_type=F32).astype(BF16)
    return jnp.concatenate([main, last], axis=0)


def down_kernel(core_ref, hidden_ref, own_ref, other_ref, send_ref):
    core = core_ref[0]
    hidden = gathered_hidden(hidden_ref)
    chips = EXPERTS // 2
    other = jnp.concatenate(
        [other_ref[...], jnp.zeros((PADDED - WIDTH, other_ref.shape[1]), BF16)], axis=0
    )
    for down, where in ((other, core), (own_ref[...], 1 - core)):
        result = lax.dot_general(hidden, down, NT, preferred_element_type=F32).astype(BF16)
        last = jnp.dot(spread(EXPERTS), result[MAIN:], preferred_element_type=F32)
        blocks = pack(result[:MAIN].astype(F32), last).reshape(chips, 2, 32, 128)
        at = pl.ds(where * chips, chips)
        send_ref[at, pl.ds(core, 1)] = blocks[:, 0:1]
        send_ref[at, pl.ds(1 - core, 1)] = blocks[:, 1:2]


def kept_kernel(back_ref, weights_ref, partial_ref):
    partial_ref[...] = lax.dot_general(
        unpack(back_ref[:, 0]), weights_ref[0], TN, preferred_element_type=F32
    )[:WIDTH]


def combine_kernel(partial_ref, came_ref, weights_ref, out_ref):
    routed = partial_ref[...]
    routed += lax.dot_general(
        unpack(came_ref[...]), weights_ref[1], TN, preferred_element_type=F32
    )[:WIDTH]
    count = out_ref.shape[1]
    out_ref[...] = (routed[:, :count] + routed[:, count:]).astype(BF16)


def call(kernel, out, **more):
    return pl.pallas_call(
        kernel,
        out_shape=out,
        compiler_params=pltpu.CompilerParams(vmem_limit_bytes=VMEM_BYTES),
        **more,
    )


def local(tokens, expert_ids, combine, w_in, w_down):
    count = tokens.shape[0]
    hidden_units = w_down.shape[1]
    core = (lax.axis_index("expert") & 1).astype(jnp.int32).reshape(1)
    everyone = ("group", "expert")
    along_z = [[x * DEPTH + z for z in range(DEPTH)] for x in range(PAIR)]
    along_plane = [
        [(x * DEPTH + z) * EXPERTS + e for x in range(PAIR) for e in range(EXPERTS)]
        for z in range(DEPTH)
    ]
    along_core = [
        [(x * DEPTH + z) * EXPERTS + 2 * y + c for x in range(PAIR) for y in range(EXPERTS // 2)]
        for z in range(DEPTH)
        for c in range(2)
    ]
    turn = [
        ((x * DEPTH + z) * EXPERTS + 2 * y + c, (c * DEPTH + z) * EXPERTS + 2 * y + 1 - x)
        for x in range(PAIR)
        for z in range(DEPTH)
        for y in range(EXPERTS // 2)
        for c in range(2)
    ]
    cores = [(e, e ^ 1) for e in range(EXPERTS)]
    tokens, ids, combine = tokens.T, expert_ids.T, combine.T
    w_in = jnp.swapaxes(w_in[0], 1, 2)
    w_down = w_down[0].T
    scalar = pl.BlockSpec(memory_space=pltpu.SMEM)
    whole = pl.BlockSpec(memory_space=pltpu.VMEM)
    anywhere = pl.BlockSpec(memory_space=pl.ANY)
    packed = (PAIR * EXPERTS, 32, 128)

    own_in = lax.ppermute(w_in, everyone, turn)
    send, mark = call(
        dispatch_kernel,
        (jax.ShapeDtypeStruct(packed, BF16), jax.ShapeDtypeStruct((8, 128), F32)),
        in_specs=[pl.BlockSpec(memory_space=pltpu.HBM)] * 2,
        scratch_shapes=[
            pltpu.VMEM(ids.shape, jnp.int32),
            pltpu.VMEM(tokens.shape, BF16),
            pltpu.SemaphoreType.DMA,
            pltpu.SemaphoreType.DMA,
        ],
    )(
        pltpu.with_memory_space_constraint(ids, pltpu.HBM),
        pltpu.with_memory_space_constraint(tokens, pltpu.HBM),
    )
    arrived = lax.all_to_all(
        send, everyone, 0, 0, axis_index_groups=along_plane, tiled=True
    )
    w_down, mark = lax.optimization_barrier((w_down, mark))
    own_in, mark = lax.optimization_barrier((own_in, mark))
    other_in = lax.ppermute(own_in, "expert", cores)
    own_down = lax.ppermute(w_down, everyone, turn)
    partial, rows = call(
        own_gate_up_kernel,
        (
            jax.ShapeDtypeStruct((SHARD * DEPTH, 2 * hidden_units), F32),
            jax.ShapeDtypeStruct((SHARD * DEPTH, PADDED), BF16),
        ),
        in_specs=[scalar, whole, anywhere],
        scratch_shapes=[pltpu.VMEM(own_in.shape, BF16), pltpu.SemaphoreType.DMA((2,))],
        cost_estimate=pl.CostEstimate(
            flops=50 * 10**9, bytes_accessed=4 * 1024 * 1024, transcendentals=0
        ),
    )(core, arrived, pltpu.with_memory_space_constraint(own_in, pltpu.HBM))
    terms = call(
        other_gate_up_kernel, jax.ShapeDtypeStruct((SHARD * DEPTH, 2 * hidden_units), BF16)
    )(partial, rows, other_in)
    sums = lax.psum_scatter(
        terms, "group", scatter_dimension=0, axis_index_groups=along_z, tiled=True
    )
    sums, own_down = lax.optimization_barrier((sums, own_down))
    other_down = lax.ppermute(own_down, "expert", cores)
    mains = EXPERTS // DEPTH * 8
    hidden = call(
        hidden_kernel, jax.ShapeDtypeStruct((DEPTH, mains, hidden_units + 128), BF16)
    )(sums)
    hidden = lax.all_to_all(hidden, "group", 0, 0, axis_index_groups=along_z, tiled=True)
    weights, own_padded = call(
        weights_kernel,
        (
            jax.ShapeDtypeStruct((PAIR, ROWS, 2 * count), BF16),
            jax.ShapeDtypeStruct((PADDED, hidden_units), BF16),
        ),
        in_specs=[scalar, whole, whole, whole, whole],
    )(core, mark, ids, combine, own_down)
    hidden, weights, own_padded = lax.optimization_barrier((hidden, weights, own_padded))
    send = call(
        down_kernel,
        jax.ShapeDtypeStruct((EXPERTS, 2, 32, 128), BF16),
        in_specs=[scalar, whole, whole, whole],
    )(core, hidden, own_padded, other_down)
    back = lax.all_to_all(send, everyone, 0, 0, axis_index_groups=along_core, tiled=True)
    came = lax.ppermute(back[:, 1], "expert", cores)
    partial = call(kept_kernel, jax.ShapeDtypeStruct((WIDTH, 2 * count), F32))(back, weights)
    routed = call(combine_kernel, jax.ShapeDtypeStruct((WIDTH, count), BF16))(
        partial, came, weights
    )
    return routed.T


def solution(mesh):
    placed = (
        P("expert", "group"),
        P("expert", None),
        P("expert", None),
        P("expert", None, None, "group"),
        P("expert", None, "group"),
    )
    return jax.shard_map(
        local, mesh=mesh, in_specs=placed, out_specs=P("expert", "group"), check_vma=False
    )
```

```python
import jax
import jax.numpy as jnp
from jax import lax
from jax.experimental import pallas as pl
from jax.experimental.pallas import tpu as pltpu
from jax.sharding import PartitionSpec as P

CAP = 18
HALF = 9
EXPERTS = 32
DEPTH = 8
PAIR = 2
WIDTH = 448
PADDED = 512
MAIN = EXPERTS * 8
ROWS = EXPERTS * HALF
SHARD = 39
F32 = jnp.float32
BF16 = jnp.bfloat16
NT = (((1,), (1,)), ((), ()))
TN = (((0,), (0,)), ((), ()))
VMEM_BYTES = 32 * 1024 * 1024


def row_of_eight(shape):
    return lax.broadcasted_iota(jnp.int32, shape, 0) & 7


def spread(count):
    row = lax.broadcasted_iota(jnp.int32, (8 * count, count), 0)
    column = lax.broadcasted_iota(jnp.int32, (8 * count, count), 1)
    return ((row >> 3) == column).astype(BF16)


def pack(main, last):
    row = row_of_eight((MAIN, 128))
    lane = lax.broadcasted_iota(jnp.int32, (MAIN, 128), 1)
    even = jnp.zeros((MAIN, 128), F32)
    odd = jnp.zeros((MAIN, 128), F32)
    for tile in range(4):
        piece = last[:, 128 * tile : 128 * tile + 128]
        even = jnp.where(row == 2 * tile, piece, even)
        odd = jnp.where(row == 2 * tile + 1, piece, odd)
    runs = odd + pltpu.roll(even, 64, 1)
    tail = jnp.where(lane < 64, main[:, 384:512], runs)
    tiles = [main[:, 128 * tile : 128 * tile + 128] for tile in range(3)] + [tail]
    return jnp.concatenate([t.reshape(EXPERTS, 8, 128) for t in tiles], axis=1).astype(BF16)


def opened(block):
    wide = block.astype(F32)
    tiles = [wide[:, 8 * tile : 8 * tile + 8, :].reshape(MAIN, 128) for tile in range(4)]
    row = row_of_eight((MAIN, 128))
    lane = lax.broadcasted_iota(jnp.int32, (MAIN, 128), 1)
    tail = tiles[3]
    main = jnp.concatenate(tiles[:3] + [jnp.where(lane < 64, tail, 0.0)], axis=1).astype(BF16)
    turned = pltpu.roll(tail, 64, 1)
    runs = [
        jnp.where(
            (row == 2 * tile) & (lane < 64),
            turned,
            jnp.where((row == 2 * tile + 1) & (lane >= 64), tail, 0.0),
        )
        for tile in range(4)
    ]
    return main, jnp.concatenate(runs, axis=1).astype(BF16)


def unpack(block):
    main, runs = opened(block)
    last = lax.dot_general(spread(EXPERTS), runs, TN, preferred_element_type=F32).astype(BF16)
    return jnp.concatenate([main, last], axis=0)


def eightfold(x):
    return jnp.broadcast_to(x[:, None, :], (x.shape[0], 8, x.shape[1])).reshape(8 * x.shape[0], x.shape[1])


def halves(rows, shift):
    index = lax.broadcasted_iota(jnp.int32, (rows, 1), 0)
    return ((index >> shift) & 1) * HALF


def labels(shape):
    index = lax.broadcasted_iota(jnp.int32, shape, 0)
    return (index & (EXPERTS - PAIR)) | (index >> 5)


def slots(ids_ref, label):
    count = ids_ref.shape[1]
    chosen = jnp.zeros(label.shape, F32)
    for pick in range(ids_ref.shape[0]):
        chosen = jnp.where(ids_ref[pick : pick + 1, :] == label, 1.0, chosen)
    before = lax.broadcasted_iota(jnp.int32, (count, count), 0) < lax.broadcasted_iota(
        jnp.int32, (count, count), 1
    )
    earlier = jnp.dot(chosen.astype(BF16), before.astype(BF16), preferred_element_type=F32)
    return jnp.where(chosen > 0.0, earlier, -1.0)


def dispatch_kernel(ids_hbm, tokens_hbm, send_ref, mark_ref, ids_ref, tokens_ref, ids_sem, tokens_sem):
    ids_copy = pltpu.make_async_copy(ids_hbm, ids_ref, ids_sem)
    tokens_copy = pltpu.make_async_copy(tokens_hbm, tokens_ref, tokens_sem)
    ids_copy.start()
    tokens_copy.start()
    count = ids_ref.shape[1]
    mark_ref[...] = jnp.zeros(mark_ref.shape, F32)
    ids_copy.wait()
    every = eightfold(slots(ids_ref, labels((PAIR * EXPERTS, count))))
    first = halves(every.shape[0], 3)
    place = (row_of_eight((every.shape[0], 1)) + first).astype(F32)
    tokens_copy.wait()
    tokens = jnp.concatenate(
        [tokens_ref[...], jnp.zeros((PADDED - WIDTH, count), BF16)], axis=0
    )
    main = (every == place).astype(BF16)
    last = (every == (first + 8).astype(F32)).astype(BF16)
    main = lax.dot_general(main, tokens, NT, preferred_element_type=F32)
    last = lax.dot_general(last, tokens, NT, preferred_element_type=F32)
    for chip in range(PAIR):
        rows = slice(MAIN * chip, MAIN * chip + MAIN)
        send_ref[EXPERTS * chip : EXPERTS * chip + EXPERTS] = pack(main[rows], last[rows])


def weights_kernel(core_ref, mark_ref, ids_ref, combine_ref, down_ref, weights_ref, padded_ref):
    del mark_ref
    padded_ref[:WIDTH] = down_ref[...]
    padded_ref[WIDTH:] = jnp.zeros((PADDED - WIDTH, down_ref.shape[1]), BF16)
    core = core_ref[0]
    index = lax.broadcasted_iota(jnp.int32, (PAIR * EXPERTS, ids_ref.shape[1]), 0)
    label = 2 * (index & 15) + ((index >> 4) & 1)
    slot = slots(ids_ref, label)
    weight = jnp.zeros(slot.shape, F32)
    for pick in range(ids_ref.shape[0]):
        weight = jnp.where(
            ids_ref[pick : pick + 1, :] == label, combine_ref[pick : pick + 1, :], weight
        )
    for part in range(PAIR):
        first = (HALF * (core if part == 0 else 1 - core)).astype(F32)
        own = slice(EXPERTS * part, EXPERTS * part + EXPERTS)
        every, each = eightfold(slot[own]), eightfold(weight[own])
        place = row_of_eight((MAIN, 1)).astype(F32) + first
        main = jnp.where(every == place, each, 0.0)
        last = jnp.where(slot[own] == first + 8.0, weight[own], 0.0)
        both = jnp.concatenate([main, last], axis=0)
        high = both.astype(BF16)
        low = (both - high.astype(F32)).astype(BF16)
        weights_ref[part] = jnp.concatenate([high, low], axis=1)


def ordered(count, blocks, column, last):
    per = count // blocks
    lasts = EXPERTS // blocks
    mains = lasts * 8
    row = lax.broadcasted_iota(jnp.int32, (count, MAIN), 0)
    block = lax.div(row, per)
    inside = row - block * per
    if last:
        chosen = (
            (inside >= mains)
            & (inside < mains + lasts)
            & ((column >> 3) == block * lasts + inside - mains)
        )
    else:
        chosen = (inside < mains) & (column == block * mains + inside)
    return chosen.astype(BF16)


def own_gate_up_kernel(core_ref, arrived_ref, own_hbm, partial_ref, rows_ref, own_ref, sems):
    copies = [
        pltpu.make_async_copy(own_hbm.at[index], own_ref.at[index], sems.at[index])
        for index in range(2)
    ]
    for copy in copies:
        copy.start()
    side = 1 - core_ref[0]
    column = lax.broadcasted_iota(jnp.int32, (SHARD * DEPTH, MAIN), 1)
    take_main = ordered(SHARD * DEPTH, DEPTH, column, False)
    take_last = ordered(SHARD * DEPTH, DEPTH, column, True)
    rows = []
    for which in (side, 1 - side):
        main, runs = opened(arrived_ref[pl.ds(which * EXPERTS, EXPERTS)])
        taken = jnp.dot(take_main, main, preferred_element_type=F32)
        taken += jnp.dot(take_last, runs, preferred_element_type=F32)
        rows.append(taken.astype(BF16))
    rows_ref[...] = rows[1]
    units = own_ref.shape[2]
    for index in range(2):
        copies[index].wait()
        for start in range(0, units, PADDED):
            part = jnp.dot(
                rows[0][:, :WIDTH],
                own_ref[index, :, start : start + PADDED],
                preferred_element_type=F32,
            )
            partial_ref[:, index * units + start : index * units + start + PADDED] = part


def other_gate_up_kernel(partial_ref, rows_ref, other_ref, terms_ref):
    units = other_ref.shape[2]
    for index in range(2):
        for start in range(0, units, PADDED):
            at = slice(index * units + start, index * units + start + PADDED)
            part = jnp.dot(
                rows_ref[:, :WIDTH],
                other_ref[index, :, start : start + PADDED],
                preferred_element_type=F32,
            )
            terms_ref[:, at] = (partial_ref[:, at] + part).astype(BF16)


def hidden_kernel(sums_ref, hidden_ref):
    units = sums_ref.shape[1] // 2
    count = sums_ref.shape[0]
    lasts = EXPERTS // DEPTH
    mains = lasts * 8
    both = sums_ref[...].astype(F32)
    gate, up = both[:, :units], both[:, units:]
    hidden = (gate / (1.0 + jnp.exp(-gate)) * up).astype(BF16)
    row = lax.broadcasted_iota(jnp.int32, (mains, count), 0)
    column = lax.broadcasted_iota(jnp.int32, (mains, count), 1)
    pick = (column == mains + lax.rem(row, lasts)).astype(BF16)
    again = jnp.dot(pick, hidden, preferred_element_type=F32)
    run = lax.div(lax.broadcasted_iota(jnp.int32, (mains, 128), 0), lasts)
    extra = jnp.zeros((mains, 128), F32)
    for tile in range(units // 128):
        extra = jnp.where(run == tile, again[:, 128 * tile : 128 * tile + 128], extra)
    block = jnp.concatenate([hidden[:mains], extra.astype(BF16)], axis=1)
    for piece in range(DEPTH):
        hidden_ref[piece] = block


def gathered_hidden(hidden_ref):
    mains = hidden_ref.shape[1]
    units = hidden_ref.shape[2] - 128
    lasts = EXPERTS // DEPTH
    main = jnp.concatenate([hidden_ref[piece, :, :units] for piece in range(DEPTH)], axis=0)
    extra = jnp.concatenate([hidden_ref[piece, :, units:] for piece in range(DEPTH)], axis=0)
    row = lax.broadcasted_iota(jnp.int32, extra.shape, 0)
    run = lax.div(lax.rem(row, mains), lasts)
    wide = extra.astype(F32)
    runs = jnp.concatenate(
        [jnp.where(run == tile, wide, 0.0) for tile in range(units // 128)], axis=1
    ).astype(BF16)
    source = lax.broadcasted_iota(jnp.int32, (EXPERTS, DEPTH * mains), 0)
    column = lax.broadcasted_iota(jnp.int32, (EXPERTS, DEPTH * mains), 1)
    pick = source == lax.div(column, mains) * lasts + lax.rem(column, lasts)
    last = jnp.dot(pick.astype(BF16), runs, preferred_element_type=F32).astype(BF16)
    return jnp.concatenate([main, last], axis=0)


def down_kernel(core_ref, hidden_ref, own_ref, other_ref, send_ref):
    core = core_ref[0]
    hidden = gathered_hidden(hidden_ref)
    chips = EXPERTS // 2
    other = jnp.concatenate(
        [other_ref[...], jnp.zeros((PADDED - WIDTH, other_ref.shape[1]), BF16)], axis=0
    )
    for down, where in ((other, core), (own_ref[...], 1 - core)):
        result = lax.dot_general(hidden, down, NT, preferred_element_type=F32).astype(BF16)
        last = jnp.dot(spread(EXPERTS), result[MAIN:], preferred_element_type=F32)
        blocks = pack(result[:MAIN].astype(F32), last).reshape(chips, 2, 32, 128)
        at = pl.ds(where * chips, chips)
        send_ref[at, pl.ds(core, 1)] = blocks[:, 0:1]
        send_ref[at, pl.ds(1 - core, 1)] = blocks[:, 1:2]


def both_parts(rows, weights):
    routed = lax.dot_general(rows, weights, TN, preferred_element_type=F32)
    count = routed.shape[1] // 2
    return routed[:, :count] + routed[:, count:]


def kept_kernel(back_ref, weights_ref, partial_ref):
    partial_ref[...] = both_parts(unpack(back_ref[:, 0]), weights_ref[0])[:WIDTH]


def combine_kernel(partial_ref, came_ref, weights_ref, out_hbm, out_ref, sems):
    rows = unpack(came_ref[...])
    copies = []
    for number, (start, stop) in enumerate(((0, 256), (256, WIDTH))):
        routed = partial_ref[start:stop] + both_parts(rows[:, start:stop], weights_ref[1])
        out_ref[start:stop] = routed.astype(BF16)
        at = pl.ds(start, stop - start)
        copies.append(pltpu.make_async_copy(out_ref.at[at], out_hbm.at[at], sems.at[number]))
        copies[number].start()
    for copy in copies:
        copy.wait()


def call(kernel, out, **more):
    return pl.pallas_call(
        kernel,
        out_shape=out,
        compiler_params=pltpu.CompilerParams(vmem_limit_bytes=VMEM_BYTES),
        **more,
    )


def local(tokens, expert_ids, combine, w_in, w_down):
    count = tokens.shape[0]
    hidden_units = w_down.shape[1]
    core = (lax.axis_index("expert") & 1).astype(jnp.int32).reshape(1)
    everyone = ("group", "expert")
    along_z = [[x * DEPTH + z for z in range(DEPTH)] for x in range(PAIR)]
    along_plane = [
        [(x * DEPTH + z) * EXPERTS + e for x in range(PAIR) for e in range(EXPERTS)]
        for z in range(DEPTH)
    ]
    along_core = [
        [(x * DEPTH + z) * EXPERTS + 2 * y + c for x in range(PAIR) for y in range(EXPERTS // 2)]
        for z in range(DEPTH)
        for c in range(2)
    ]
    turn = [
        ((x * DEPTH + z) * EXPERTS + 2 * y + c, (c * DEPTH + z) * EXPERTS + 2 * y + 1 - x)
        for x in range(PAIR)
        for z in range(DEPTH)
        for y in range(EXPERTS // 2)
        for c in range(2)
    ]
    cores = [(e, e ^ 1) for e in range(EXPERTS)]
    tokens, ids, combine = tokens.T, expert_ids.T, combine.T
    w_in = jnp.swapaxes(w_in[0], 1, 2)
    w_down = w_down[0].T
    scalar = pl.BlockSpec(memory_space=pltpu.SMEM)
    whole = pl.BlockSpec(memory_space=pltpu.VMEM)
    anywhere = pl.BlockSpec(memory_space=pl.ANY)
    packed = (PAIR * EXPERTS, 32, 128)

    own_in = lax.ppermute(w_in, everyone, turn)
    send, mark = call(
        dispatch_kernel,
        (jax.ShapeDtypeStruct(packed, BF16), jax.ShapeDtypeStruct((8, 128), F32)),
        in_specs=[pl.BlockSpec(memory_space=pltpu.HBM)] * 2,
        scratch_shapes=[
            pltpu.VMEM(ids.shape, jnp.int32),
            pltpu.VMEM(tokens.shape, BF16),
            pltpu.SemaphoreType.DMA,
            pltpu.SemaphoreType.DMA,
        ],
    )(
        pltpu.with_memory_space_constraint(ids, pltpu.HBM),
        pltpu.with_memory_space_constraint(tokens, pltpu.HBM),
    )
    arrived = lax.all_to_all(
        send, everyone, 0, 0, axis_index_groups=along_plane, tiled=True
    )
    w_down, mark = lax.optimization_barrier((w_down, mark))
    own_in, mark = lax.optimization_barrier((own_in, mark))
    other_in = lax.ppermute(own_in, "expert", cores)
    own_down = lax.ppermute(w_down, everyone, turn)
    partial, rows = call(
        own_gate_up_kernel,
        (
            jax.ShapeDtypeStruct((SHARD * DEPTH, 2 * hidden_units), F32),
            jax.ShapeDtypeStruct((SHARD * DEPTH, PADDED), BF16),
        ),
        in_specs=[scalar, whole, anywhere],
        scratch_shapes=[pltpu.VMEM(own_in.shape, BF16), pltpu.SemaphoreType.DMA((2,))],
        cost_estimate=pl.CostEstimate(
            flops=50 * 10**9, bytes_accessed=4 * 1024 * 1024, transcendentals=0
        ),
    )(core, arrived, pltpu.with_memory_space_constraint(own_in, pltpu.HBM))
    terms = call(
        other_gate_up_kernel, jax.ShapeDtypeStruct((SHARD * DEPTH, 2 * hidden_units), BF16)
    )(partial, rows, other_in)
    sums = lax.psum_scatter(
        terms, "group", scatter_dimension=0, axis_index_groups=along_z, tiled=True
    )
    sums, own_down = lax.optimization_barrier((sums, own_down))
    other_down = lax.ppermute(own_down, "expert", cores)
    mains = EXPERTS // DEPTH * 8
    hidden = call(
        hidden_kernel, jax.ShapeDtypeStruct((DEPTH, mains, hidden_units + 128), BF16)
    )(sums)
    hidden = lax.all_to_all(hidden, "group", 0, 0, axis_index_groups=along_z, tiled=True)
    weights, own_padded = call(
        weights_kernel,
        (
            jax.ShapeDtypeStruct((PAIR, ROWS, 2 * count), BF16),
            jax.ShapeDtypeStruct((PADDED, hidden_units), BF16),
        ),
        in_specs=[scalar, whole, whole, whole, whole],
    )(core, mark, ids, combine, own_down)
    hidden, weights, own_padded = lax.optimization_barrier((hidden, weights, own_padded))
    send = call(
        down_kernel,
        jax.ShapeDtypeStruct((EXPERTS, 2, 32, 128), BF16),
        in_specs=[scalar, whole, whole, whole],
    )(core, hidden, own_padded, other_down)
    back = lax.all_to_all(send, everyone, 0, 0, axis_index_groups=along_core, tiled=True)
    came = lax.ppermute(back[:, 1], "expert", cores)
    partial = call(kept_kernel, jax.ShapeDtypeStruct((WIDTH, count), F32))(back, weights)
    routed = call(
        combine_kernel,
        jax.ShapeDtypeStruct((WIDTH, count), BF16),
        out_specs=anywhere,
        scratch_shapes=[pltpu.VMEM((WIDTH, count), BF16), pltpu.SemaphoreType.DMA((2,))],
    )(partial, came, weights)
    return routed.T


def solution(mesh):
    placed = (
        P("expert", "group"),
        P("expert", None),
        P("expert", None),
        P("expert", None, None, "group"),
        P("expert", None, "group"),
    )
    return jax.shard_map(
        local, mesh=mesh, in_specs=placed, out_specs=P("expert", "group"), check_vma=False
    )
```

```python
import jax
import jax.numpy as jnp
from jax import lax
from jax.experimental import pallas as pl
from jax.experimental.pallas import tpu as pltpu
from jax.sharding import PartitionSpec as P

CAP = 18
HALF = 9
EXPERTS = 32
DEPTH = 8
PAIR = 2
WIDTH = 448
PADDED = 512
MAIN = EXPERTS * 8
ROWS = EXPERTS * HALF
SHARD = 39
F32 = jnp.float32
BF16 = jnp.bfloat16
NT = (((1,), (1,)), ((), ()))
TN = (((0,), (0,)), ((), ()))
VMEM_BYTES = 32 * 1024 * 1024


def row_of_eight(shape):
    return lax.broadcasted_iota(jnp.int32, shape, 0) & 7


def spread(count):
    row = lax.broadcasted_iota(jnp.int32, (8 * count, count), 0)
    column = lax.broadcasted_iota(jnp.int32, (8 * count, count), 1)
    return ((row >> 3) == column).astype(BF16)


def pack(main, last):
    row = row_of_eight((MAIN, 128))
    lane = lax.broadcasted_iota(jnp.int32, (MAIN, 128), 1)
    even = jnp.zeros((MAIN, 128), F32)
    odd = jnp.zeros((MAIN, 128), F32)
    for tile in range(4):
        piece = last[:, 128 * tile : 128 * tile + 128]
        even = jnp.where(row == 2 * tile, piece, even)
        odd = jnp.where(row == 2 * tile + 1, piece, odd)
    runs = odd + pltpu.roll(even, 64, 1)
    tail = jnp.where(lane < 64, main[:, 384:512], runs)
    tiles = [main[:, 128 * tile : 128 * tile + 128] for tile in range(3)] + [tail]
    return jnp.concatenate([t.reshape(EXPERTS, 8, 128) for t in tiles], axis=1).astype(BF16)


def opened(block):
    wide = block.astype(F32)
    tiles = [wide[:, 8 * tile : 8 * tile + 8, :].reshape(MAIN, 128) for tile in range(4)]
    row = row_of_eight((MAIN, 128))
    lane = lax.broadcasted_iota(jnp.int32, (MAIN, 128), 1)
    tail = tiles[3]
    main = jnp.concatenate(tiles[:3] + [jnp.where(lane < 64, tail, 0.0)], axis=1).astype(BF16)
    turned = pltpu.roll(tail, 64, 1)
    runs = [
        jnp.where(
            (row == 2 * tile) & (lane < 64),
            turned,
            jnp.where((row == 2 * tile + 1) & (lane >= 64), tail, 0.0),
        )
        for tile in range(4)
    ]
    return main, jnp.concatenate(runs, axis=1).astype(BF16)


def unpack(block):
    main, runs = opened(block)
    last = lax.dot_general(spread(EXPERTS), runs, TN, preferred_element_type=F32).astype(BF16)
    return jnp.concatenate([main, last], axis=0)


def eightfold(x):
    return jnp.broadcast_to(x[:, None, :], (x.shape[0], 8, x.shape[1])).reshape(8 * x.shape[0], x.shape[1])


def halves(rows, shift):
    index = lax.broadcasted_iota(jnp.int32, (rows, 1), 0)
    return ((index >> shift) & 1) * HALF


def labels(shape):
    index = lax.broadcasted_iota(jnp.int32, shape, 0)
    return (index & (EXPERTS - PAIR)) | (index >> 5)


def slots(ids_ref, label):
    count = ids_ref.shape[1]
    chosen = jnp.zeros(label.shape, F32)
    for pick in range(ids_ref.shape[0]):
        chosen = jnp.where(ids_ref[pick : pick + 1, :] == label, 1.0, chosen)
    before = lax.broadcasted_iota(jnp.int32, (count, count), 0) < lax.broadcasted_iota(
        jnp.int32, (count, count), 1
    )
    earlier = jnp.dot(chosen.astype(BF16), before.astype(BF16), preferred_element_type=F32)
    return jnp.where(chosen > 0.0, earlier, -1.0)


def dispatch_kernel(ids_hbm, tokens_hbm, send_ref, mark_ref, ids_ref, tokens_ref, ids_sem, tokens_sem):
    ids_copy = pltpu.make_async_copy(ids_hbm, ids_ref, ids_sem)
    tokens_copy = pltpu.make_async_copy(tokens_hbm, tokens_ref, tokens_sem)
    ids_copy.start()
    tokens_copy.start()
    count = ids_ref.shape[1]
    mark_ref[...] = jnp.zeros(mark_ref.shape, F32)
    ids_copy.wait()
    every = eightfold(slots(ids_ref, labels((PAIR * EXPERTS, count))))
    first = halves(every.shape[0], 3)
    place = (row_of_eight((every.shape[0], 1)) + first).astype(F32)
    tokens_copy.wait()
    tokens = jnp.concatenate(
        [tokens_ref[...], jnp.zeros((PADDED - WIDTH, count), BF16)], axis=0
    )
    main = (every == place).astype(BF16)
    last = (every == (first + 8).astype(F32)).astype(BF16)
    main = lax.dot_general(main, tokens, NT, preferred_element_type=F32)
    last = lax.dot_general(last, tokens, NT, preferred_element_type=F32)
    for chip in range(PAIR):
        rows = slice(MAIN * chip, MAIN * chip + MAIN)
        send_ref[EXPERTS * chip : EXPERTS * chip + EXPERTS] = pack(main[rows], last[rows])


def weights_kernel(core_ref, mark_ref, ids_ref, combine_ref, down_ref, weights_ref, padded_ref):
    del mark_ref
    padded_ref[:WIDTH] = down_ref[...]
    padded_ref[WIDTH:] = jnp.zeros((PADDED - WIDTH, down_ref.shape[1]), BF16)
    core = core_ref[0]
    index = lax.broadcasted_iota(jnp.int32, (PAIR * EXPERTS, ids_ref.shape[1]), 0)
    label = 2 * (index & 15) + ((index >> 4) & 1)
    slot = slots(ids_ref, label)
    weight = jnp.zeros(slot.shape, F32)
    for pick in range(ids_ref.shape[0]):
        weight = jnp.where(
            ids_ref[pick : pick + 1, :] == label, combine_ref[pick : pick + 1, :], weight
        )
    for part in range(PAIR):
        first = (HALF * (core if part == 0 else 1 - core)).astype(F32)
        own = slice(EXPERTS * part, EXPERTS * part + EXPERTS)
        every, each = eightfold(slot[own]), eightfold(weight[own])
        place = row_of_eight((MAIN, 1)).astype(F32) + first
        main = jnp.where(every == place, each, 0.0)
        last = jnp.where(slot[own] == first + 8.0, weight[own], 0.0)
        both = jnp.concatenate([main, last], axis=0)
        high = both.astype(BF16)
        low = (both - high.astype(F32)).astype(BF16)
        weights_ref[part] = jnp.concatenate([high, low], axis=1)


def ordered(count, blocks, column, last):
    per = count // blocks
    lasts = EXPERTS // blocks
    mains = lasts * 8
    row = lax.broadcasted_iota(jnp.int32, (count, MAIN), 0)
    block = lax.div(row, per)
    inside = row - block * per
    if last:
        chosen = (
            (inside >= mains)
            & (inside < mains + lasts)
            & ((column >> 3) == block * lasts + inside - mains)
        )
    else:
        chosen = (inside < mains) & (column == block * mains + inside)
    return chosen.astype(BF16)


def own_gate_up_kernel(core_ref, arrived_ref, own_hbm, partial_ref, rows_ref, own_ref, sems):
    copies = [
        pltpu.make_async_copy(own_hbm.at[index], own_ref.at[index], sems.at[index])
        for index in range(2)
    ]
    for copy in copies:
        copy.start()
    side = 1 - core_ref[0]
    column = lax.broadcasted_iota(jnp.int32, (SHARD * DEPTH, MAIN), 1)
    take_main = ordered(SHARD * DEPTH, DEPTH, column, False)
    take_last = ordered(SHARD * DEPTH, DEPTH, column, True)
    rows = []
    for which in (side, 1 - side):
        main, runs = opened(arrived_ref[pl.ds(which * EXPERTS, EXPERTS)])
        taken = jnp.dot(take_main, main, preferred_element_type=F32)
        taken += jnp.dot(take_last, runs, preferred_element_type=F32)
        rows.append(taken.astype(BF16))
    rows_ref[...] = rows[1]
    units = own_ref.shape[2]
    for index in range(2):
        copies[index].wait()
        for start in range(0, units, PADDED):
            part = jnp.dot(
                rows[0][:, :WIDTH],
                own_ref[index, :, start : start + PADDED],
                preferred_element_type=F32,
            )
            partial_ref[:, index * units + start : index * units + start + PADDED] = part


def other_gate_up_kernel(partial_ref, rows_ref, other_ref, terms_ref):
    units = other_ref.shape[2]
    for index in range(2):
        for start in range(0, units, PADDED):
            at = slice(index * units + start, index * units + start + PADDED)
            part = jnp.dot(
                rows_ref[:, :WIDTH],
                other_ref[index, :, start : start + PADDED],
                preferred_element_type=F32,
            )
            terms_ref[:, at] = (partial_ref[:, at] + part).astype(BF16)


def hidden_kernel(sums_ref, hidden_ref):
    units = sums_ref.shape[1] // 2
    count = sums_ref.shape[0]
    lasts = EXPERTS // DEPTH
    mains = lasts * 8
    both = sums_ref[...].astype(F32)
    gate, up = both[:, :units], both[:, units:]
    hidden = (gate / (1.0 + jnp.exp(-gate)) * up).astype(BF16)
    row = lax.broadcasted_iota(jnp.int32, (mains, count), 0)
    column = lax.broadcasted_iota(jnp.int32, (mains, count), 1)
    pick = (column == mains + lax.rem(row, lasts)).astype(BF16)
    again = jnp.dot(pick, hidden, preferred_element_type=F32)
    run = lax.div(lax.broadcasted_iota(jnp.int32, (mains, 128), 0), lasts)
    extra = jnp.zeros((mains, 128), F32)
    for tile in range(units // 128):
        extra = jnp.where(run == tile, again[:, 128 * tile : 128 * tile + 128], extra)
    block = jnp.concatenate([hidden[:mains], extra.astype(BF16)], axis=1)
    for piece in range(DEPTH):
        hidden_ref[piece] = block


def gathered_hidden(hidden_ref):
    mains = hidden_ref.shape[1]
    units = hidden_ref.shape[2] - 128
    lasts = EXPERTS // DEPTH
    main = jnp.concatenate([hidden_ref[piece, :, :units] for piece in range(DEPTH)], axis=0)
    extra = jnp.concatenate([hidden_ref[piece, :, units:] for piece in range(DEPTH)], axis=0)
    row = lax.broadcasted_iota(jnp.int32, extra.shape, 0)
    run = lax.div(lax.rem(row, mains), lasts)
    wide = extra.astype(F32)
    runs = jnp.concatenate(
        [jnp.where(run == tile, wide, 0.0) for tile in range(units // 128)], axis=1
    ).astype(BF16)
    source = lax.broadcasted_iota(jnp.int32, (EXPERTS, DEPTH * mains), 0)
    column = lax.broadcasted_iota(jnp.int32, (EXPERTS, DEPTH * mains), 1)
    pick = source == lax.div(column, mains) * lasts + lax.rem(column, lasts)
    last = jnp.dot(pick.astype(BF16), runs, preferred_element_type=F32).astype(BF16)
    return jnp.concatenate([main, last], axis=0)


def down_kernel(core_ref, hidden_ref, own_ref, other_ref, send_ref):
    core = core_ref[0]
    hidden = gathered_hidden(hidden_ref)
    chips = EXPERTS // 2
    whole_tiles = WIDTH // 128 * 128
    tail = jnp.concatenate(
        [other_ref[whole_tiles:], jnp.zeros((PADDED - WIDTH, other_ref.shape[1]), BF16)], axis=0
    )
    for downs, where in (((other_ref[:whole_tiles], tail), core), ((own_ref[...],), 1 - core)):
        result = [
            lax.dot_general(hidden, down, NT, preferred_element_type=F32) for down in downs
        ]
        result = jnp.concatenate(result, axis=1).astype(BF16)
        last = jnp.dot(spread(EXPERTS), result[MAIN:], preferred_element_type=F32)
        blocks = pack(result[:MAIN].astype(F32), last).reshape(chips, 2, 32, 128)
        at = pl.ds(where * chips, chips)
        send_ref[at, pl.ds(core, 1)] = blocks[:, 0:1]
        send_ref[at, pl.ds(1 - core, 1)] = blocks[:, 1:2]


def both_parts(rows, weights):
    routed = lax.dot_general(rows, weights, TN, preferred_element_type=F32)
    count = routed.shape[1] // 2
    return routed[:, :count] + routed[:, count:]


def kept_kernel(back_ref, weights_ref, partial_ref):
    partial_ref[...] = both_parts(unpack(back_ref[:, 0]), weights_ref[0])[:WIDTH]


def combine_kernel(partial_ref, came_ref, weights_ref, out_hbm, out_ref, sems):
    rows = unpack(came_ref[...])
    copies = []
    for number, (start, stop) in enumerate(((0, 256), (256, WIDTH))):
        routed = partial_ref[start:stop] + both_parts(rows[:, start:stop], weights_ref[1])
        out_ref[start:stop] = routed.astype(BF16)
        at = pl.ds(start, stop - start)
        copies.append(pltpu.make_async_copy(out_ref.at[at], out_hbm.at[at], sems.at[number]))
        copies[number].start()
    for copy in copies:
        copy.wait()


def call(kernel, out, **more):
    return pl.pallas_call(
        kernel,
        out_shape=out,
        compiler_params=pltpu.CompilerParams(vmem_limit_bytes=VMEM_BYTES),
        **more,
    )


def local(tokens, expert_ids, combine, w_in, w_down):
    count = tokens.shape[0]
    hidden_units = w_down.shape[1]
    core = (lax.axis_index("expert") & 1).astype(jnp.int32).reshape(1)
    everyone = ("group", "expert")
    along_z = [[x * DEPTH + z for z in range(DEPTH)] for x in range(PAIR)]
    along_plane = [
        [(x * DEPTH + z) * EXPERTS + e for x in range(PAIR) for e in range(EXPERTS)]
        for z in range(DEPTH)
    ]
    along_core = [
        [(x * DEPTH + z) * EXPERTS + 2 * y + c for x in range(PAIR) for y in range(EXPERTS // 2)]
        for z in range(DEPTH)
        for c in range(2)
    ]
    turn = [
        ((x * DEPTH + z) * EXPERTS + 2 * y + c, (c * DEPTH + z) * EXPERTS + 2 * y + 1 - x)
        for x in range(PAIR)
        for z in range(DEPTH)
        for y in range(EXPERTS // 2)
        for c in range(2)
    ]
    cores = [(e, e ^ 1) for e in range(EXPERTS)]
    tokens, ids, combine = tokens.T, expert_ids.T, combine.T
    w_in = jnp.swapaxes(w_in[0], 1, 2)
    w_down = w_down[0].T
    scalar = pl.BlockSpec(memory_space=pltpu.SMEM)
    whole = pl.BlockSpec(memory_space=pltpu.VMEM)
    anywhere = pl.BlockSpec(memory_space=pl.ANY)
    packed = (PAIR * EXPERTS, 32, 128)

    own_in = lax.ppermute(w_in, everyone, turn)
    send, mark = call(
        dispatch_kernel,
        (jax.ShapeDtypeStruct(packed, BF16), jax.ShapeDtypeStruct((8, 128), F32)),
        in_specs=[pl.BlockSpec(memory_space=pltpu.HBM)] * 2,
        scratch_shapes=[
            pltpu.VMEM(ids.shape, jnp.int32),
            pltpu.VMEM(tokens.shape, BF16),
            pltpu.SemaphoreType.DMA,
            pltpu.SemaphoreType.DMA,
        ],
    )(
        pltpu.with_memory_space_constraint(ids, pltpu.HBM),
        pltpu.with_memory_space_constraint(tokens, pltpu.HBM),
    )
    arrived = lax.all_to_all(
        send, everyone, 0, 0, axis_index_groups=along_plane, tiled=True
    )
    w_down, mark = lax.optimization_barrier((w_down, mark))
    own_in, mark = lax.optimization_barrier((own_in, mark))
    other_in = lax.ppermute(own_in, "expert", cores)
    own_down = lax.ppermute(w_down, everyone, turn)
    partial, rows = call(
        own_gate_up_kernel,
        (
            jax.ShapeDtypeStruct((SHARD * DEPTH, 2 * hidden_units), F32),
            jax.ShapeDtypeStruct((SHARD * DEPTH, PADDED), BF16),
        ),
        in_specs=[scalar, whole, anywhere],
        scratch_shapes=[pltpu.VMEM(own_in.shape, BF16), pltpu.SemaphoreType.DMA((2,))],
        cost_estimate=pl.CostEstimate(
            flops=50 * 10**9, bytes_accessed=4 * 1024 * 1024, transcendentals=0
        ),
    )(core, arrived, pltpu.with_memory_space_constraint(own_in, pltpu.HBM))
    terms = call(
        other_gate_up_kernel, jax.ShapeDtypeStruct((SHARD * DEPTH, 2 * hidden_units), BF16)
    )(partial, rows, other_in)
    sums = lax.psum_scatter(
        terms, "group", scatter_dimension=0, axis_index_groups=along_z, tiled=True
    )
    sums, own_down = lax.optimization_barrier((sums, own_down))
    other_down = lax.ppermute(own_down, "expert", cores)
    mains = EXPERTS // DEPTH * 8
    hidden = call(
        hidden_kernel, jax.ShapeDtypeStruct((DEPTH, mains, hidden_units + 128), BF16)
    )(sums)
    hidden = lax.all_to_all(hidden, "group", 0, 0, axis_index_groups=along_z, tiled=True)
    weights, own_padded = call(
        weights_kernel,
        (
            jax.ShapeDtypeStruct((PAIR, ROWS, 2 * count), BF16),
            jax.ShapeDtypeStruct((PADDED, hidden_units), BF16),
        ),
        in_specs=[scalar, whole, whole, whole, whole],
    )(core, mark, ids, combine, own_down)
    hidden, weights, own_padded = lax.optimization_barrier((hidden, weights, own_padded))
    send = call(
        down_kernel,
        jax.ShapeDtypeStruct((EXPERTS, 2, 32, 128), BF16),
        in_specs=[scalar, whole, whole, whole],
    )(core, hidden, own_padded, other_down)
    back = lax.all_to_all(send, everyone, 0, 0, axis_index_groups=along_core, tiled=True)
    came = lax.ppermute(back[:, 1], "expert", cores)
    partial = call(kept_kernel, jax.ShapeDtypeStruct((WIDTH, count), F32))(back, weights)
    routed = call(
        combine_kernel,
        jax.ShapeDtypeStruct((WIDTH, count), BF16),
        out_specs=anywhere,
        scratch_shapes=[pltpu.VMEM((WIDTH, count), BF16), pltpu.SemaphoreType.DMA((2,))],
    )(partial, came, weights)
    return routed.T


def solution(mesh):
    placed = (
        P("expert", "group"),
        P("expert", None),
        P("expert", None),
        P("expert", None, None, "group"),
        P("expert", None, "group"),
    )
    return jax.shard_map(
        local, mesh=mesh, in_specs=placed, out_specs=P("expert", "group"), check_vma=False
    )
```
